256 devices in a mesh: row: 16 (over z_hi, y), col: 16 (over z_lo, x, core).
Axes of the slice: x: 4, y: 4, z: 8 (z_hi: 4, z_lo: 2; z = z_hi * 2 + z_lo), core: 2. Of those that a mesh axis runs over, the one named last changes fastest.
Arguments:
- out_grad: bfloat16 [65536, 128], P(('row', 'col')), may hold values from -6 to 6
- preact: bfloat16 [65536, 128], P(('row', 'col')), may hold values from -6 to 6
- aggregated: bfloat16 [65536, 128], P(('row', 'col')), may hold values from -6 to 6
- weight: bfloat16 [128, 128], replicated, may hold values from -0.5 to 0.5
- tiles: bfloat16 [16, 16, 256, 128, 128], P('row', 'col'), may hold values from -0.09375 to 0.09375
- tile_coords: int32 [16, 16, 2, 256], P('row', 'col'), may hold values from 0 to 31, as said below
- tile_count: int32 [16, 16], P('row', 'col'), may hold values from 32 to 256, as said below
Outputs:
- input_grad: bfloat16 [65536, 128], P(('row', 'col'))
- weight_grad: float32 [128, 128], replicated
The draws below stay inside these ranges and needn't reach their ends.
Inputs may be any that keep to these rules, and one draw needn't show every extreme that they name: `tile_coords`: on each device the first tile_count slots hold distinct tiles, in non-decreasing row block; row blocks are below 32 and column blocks below 32; entries of later slots are not used. `tile_count`: some device uses all 256 slots.
All inputs are finite; a program needn't handle non-finite values.
Results may differ from the reference program's by a relative error of at most 0.0049.
Values may be sent and summed in bfloat16 or wider, within the bound.
No kernel may reach another device: no remote copies, remote signals or barrier semaphores. Data moves between devices by JAX's collectives and lax.ppermute only.
A program may use at most 64 MiB of HBM per device.

```python
import math
import jax
import jax.numpy as jnp
from jax import lax

F = 128
NODE_DEV = 256
BLK = 128
TILE_ROW = 8
NODES = 65536
ROWBLK = 32
COLBLK = 32
TILES_DEV = 256
N_ROW = 16
N_COL = 16


def tile_layout(key):
    count_key, other_key, place_key, perm_key = jax.random.split(key, 4)
    devices = N_ROW * N_COL
    first_draw = jax.random.randint(count_key, (devices,), 0, TILES_DEV + 1)
    second_draw = jax.random.randint(other_key, (devices,), 0, TILES_DEV + 1)
    counts = jnp.maximum(TILES_DEV // 8, first_draw * second_draw // TILES_DEV)
    fullest = jax.random.randint(place_key, (), 0, devices)
    counts = jnp.where(jnp.arange(devices) == fullest, TILES_DEV, counts).astype(jnp.int32)
    cells = ROWBLK * COLBLK
    perm_keys = jax.random.split(perm_key, devices)
    chosen = jax.vmap(lambda one_key: jax.random.permutation(one_key, cells))(perm_keys)[:, :TILES_DEV]
    slot_ids = jnp.arange(TILES_DEV)
    ordered = jnp.where(slot_ids[None, :] < counts[:, None], chosen, chosen + cells)
    ordered = jnp.sort(ordered, axis=1) % cells
    return (counts, ordered.astype(jnp.int32))


def draw_tile_coords(key, part):
    counts, ordered = tile_layout(key)
    row_blocks = ordered // COLBLK
    col_blocks = ordered % COLBLK
    stacked = jnp.stack([row_blocks, col_blocks], axis=1)
    return stacked.reshape(N_ROW, N_COL, 2, TILES_DEV).astype(jnp.int32)


def draw_tile_count(key, part):
    counts, ordered = tile_layout(key)
    return counts.reshape(N_ROW, N_COL).astype(jnp.int32)


def block_levels(stream_key, shape, cuts, least, largest):
    level = 1.0
    for axis_at, blocks in cuts:
        steps = jax.random.uniform(jax.random.fold_in(jax.random.fold_in(stream_key, 6), axis_at), (blocks,), jnp.float32, least / len(cuts), largest / len(cuts))
        level = level * jnp.repeat(jnp.exp(steps), shape[axis_at] // blocks).reshape((-1,) + (1,) * (len(shape) - 1 - axis_at))
    return level


def noise(own_key, shape, spread, most, shards=(), kind=jnp.bfloat16):
    entries = spread * jax.random.normal(own_key, shape, jnp.float32)
    if shards:
        entries = entries * block_levels(own_key, shape, shards, -0.22, 0.18)
    return jnp.clip(entries, -most, most).astype(kind)


def setup_inputs(seed: int = 0) -> dict:
    keys = jax.random.split(jax.random.key(seed), 8)
    return {
        "out_grad": noise(keys[0], (NODES, F), 1.0, 6.0, ((0, 256),)),
        "preact": noise(keys[1], (NODES, F), 1.0, 6.0, ((0, 256),)),
        "aggregated": noise(keys[2], (NODES, F), 1.0, 6.0, ((0, 256),)),
        "weight": noise(keys[3], (F, F), F ** -0.5, 0.5),
        "tiles": noise(keys[4], (N_ROW, N_COL, TILES_DEV, BLK, BLK), (N_ROW * TILE_ROW * BLK * ROWBLK // (4 * COLBLK)) ** -0.5, 0.09375, ((0, 16), (1, 16))),
        "tile_coords": draw_tile_coords(jax.random.fold_in(keys[7], 71), 0),
        "tile_count": draw_tile_count(jax.random.fold_in(keys[7], 71), 0),
    }


def reference(out_grad, preact, aggregated, weight, tiles, tile_coords, tile_count):
    grad_pre = jnp.where(preact > 0, out_grad, jnp.zeros_like(out_grad))
    weight_grad = jnp.dot(aggregated.T, grad_pre, preferred_element_type=jnp.float32) * (1.0 / math.sqrt(NODES))
    grad_agg = jnp.dot(grad_pre, weight.T, preferred_element_type=jnp.float32).astype(jnp.bfloat16)
    per_shard = NODE_DEV // BLK
    agg_blocks = grad_agg.reshape(NODES // BLK, BLK, F)
    devices = N_ROW * N_COL
    flat_tiles = tiles.reshape(devices, TILES_DEV, BLK, BLK)
    flat_coords = tile_coords.reshape(devices, 2, TILES_DEV)
    flat_count = tile_count.reshape(devices)
    device_ids = jnp.arange(devices, dtype=jnp.int32)
    slot_ids = jnp.arange(TILES_DEV, dtype=jnp.int32)

    def one_device(running_sum, inputs):
        tile_vals, coords, in_use, device = inputs
        row_group = device // N_COL
        col_group = device % N_COL
        global_rows = (row_group * ROWBLK + coords[0]).astype(jnp.int32)
        local_cols = coords[1]
        global_cols = ((local_cols // per_shard * N_COL + col_group) * per_shard + local_cols % per_shard).astype(jnp.int32)
        live = (slot_ids < in_use).astype(jnp.float32)
        sources = agg_blocks[global_rows].astype(jnp.float32)
        products = jnp.einsum('tab,taf->tbf', tile_vals.astype(jnp.float32), sources) * live[:, None, None]
        return (running_sum.at[global_cols].add(products), None)
    start_sum = jnp.zeros((NODES // BLK, BLK, F), jnp.float32)
    total, _unused = lax.scan(one_device, start_sum, (flat_tiles, flat_coords, flat_count, device_ids))
    return (total.reshape(NODES, F).astype(jnp.bfloat16), weight_grad)
```

```python
import functools
import itertools

import jax
import jax.numpy as jnp
from jax import lax
from jax.experimental import pallas as pl
from jax.experimental.pallas import tpu as pltpu
from jax.sharding import Mesh, PartitionSpec as P

bf16 = jnp.bfloat16
f32 = jnp.float32
T = 128
ROWS = ("zh", "y")
COLS = ("zl", "x", "core")
GROUP = 16
UNROLL = 8
LIMIT = 48 * 1024 * 1024

PEERS = [(dz, dx) for dz in range(2) for dx in range(4)]


def spec(space=pltpu.VMEM):
    return pl.BlockSpec(memory_space=space)


def split_parts(value):
    high = value.astype(bf16)
    low = (value - high.astype(f32)).astype(bf16)
    return high, low


def join_parts(high, low):
    return high.astype(f32) + low.astype(f32)


def ring_sum(own, received):
    return (own + received[1]) + (received[0] + received[2])


def prep_kernel(pos, og, pre, agg, weight, *refs):
    messages, wbuf = refs[:8], refs[8]
    zl, x = pos[2], pos[3]
    grad_pre = jnp.where(pre[...] > 0, og[...], jnp.zeros_like(og))
    g_t = lax.dot_general(
        weight[...], grad_pre, (((1,), (1,)), ((), ())), preferred_element_type=f32
    ).astype(bf16)
    wbuf[...] = lax.dot_general(
        agg[...], grad_pre, (((0,), (0,)), ((), ())), preferred_element_type=f32
    )
    for (dz, dx), message in zip(PEERS, messages):
        target = ((zl + dz) % 2) * 4 + (x + dx) % 4
        high, low = split_parts(wbuf[pl.ds(pl.multiple_of(target * 16, 16), 16), :])
        message[0:T, :] = g_t
        message[T : T + 16, 0:T] = high
        message[T : T + 16, T : 2 * T] = low


def tile_kernel(pos, count_ref, coords, *refs):
    own, other = refs[0:8], refs[8:16]
    tiles = refs[16]
    keep, keep_w, sends = refs[17], refs[18], refs[19:22]
    tile_buf, grads, acc, sems = refs[22:]
    y, zl, x, core = pos[1], pos[2], pos[3], pos[4]
    count = count_ref[0]
    slots = tiles.shape[0]

    def fetch(group):
        part = pl.ds(group * GROUP, GROUP)
        return pltpu.make_async_copy(tiles.at[part], tile_buf.at[part], sems.at[group])

    for group in range(slots // GROUP):

        @pl.when(group * GROUP < count)
        def _():
            fetch(group).start()

    sums = [jnp.zeros((16, T), f32)] * 2
    for i, (dz, dx) in enumerate(PEERS):
        shard = ((zl + 2 - dz) % 2) * 4 + (x + 4 - dx) % 4
        for side, (message, at) in enumerate(((own[i], core), (other[i], 1 - core))):
            base = (shard * 2 + at) * 2
            grads[base] = message[0:T, 0:T]
            grads[base + 1] = message[0:T, T : 2 * T]
            sums[side] += join_parts(message[T : T + 16, 0:T], message[T : T + 16, T : 2 * T])

    acc[...] = jnp.zeros_like(acc)
    dump = acc.shape[0] - 1

    @pl.loop(0, (count + GROUP - 1) // GROUP)
    def _(group):
        fetch(group).wait()

        @pl.loop(0, GROUP // UNROLL)
        def _(part):
            for u in range(UNROLL):
                k = group * GROUP + part * UNROLL + u
                live = k < count
                p = jnp.where(live, coords[0, k], 0)
                q = jnp.where(live, coords[1, k], dump)
                acc[q] += jnp.dot(grads[p], tile_buf[k], preferred_element_type=f32)

    high, low = split_parts(sums[0] + sums[1])
    for d in range(4):
        for zh in range(4):
            for h in range(2):
                q = (zh * 4 + (y + d) % 4) * 2 + h
                rows = pl.ds((zh * 2 + h) * T, T)
                if d == 0:
                    keep[rows, :] = acc[q]
                else:
                    sends[d - 1][rows, :] = acc[q].astype(bf16)
        if d:
            sends[d - 1][1024:1040, :] = high
            sends[d - 1][1040:1056, :] = low
    keep_w[...] = join_parts(high, low)


def y_kernel(pos, keep, keep_w, r1, r2, r3, keep_z, keep_zw, s1, s2, s3):
    zh_me = pos[0]
    parts = [join_parts(r[1024:1040, :], r[1040:1056, :]) for r in (r1, r2, r3)]
    high, low = split_parts(ring_sum(keep_w[...], parts))
    keep_zw[...] = join_parts(high, low)
    for d, out in enumerate((keep_z, s1, s2, s3)):
        rows = pl.ds(pl.multiple_of(((zh_me + d) % 4) * 256, 256), 256)
        total = keep[rows, :]
        for r in (r1, r2, r3):
            total += r[rows, :].astype(f32)
        if d == 0:
            out[...] = total
        else:
            out[0:256, :] = total.astype(bf16)
            out[256:272, :] = high
            out[272:288, :] = low


def z_kernel(keep_z, keep_zw, r1, r2, r3, out, chunk_out):
    parts = [join_parts(r[256:272, :], r[272:288, :]) for r in (r1, r2, r3)]
    chunk_out[...] = ring_sum(keep_zw[...], parts)
    for h in range(2):
        rows = pl.ds(h * T, T)
        total = keep_z[rows, :]
        for r in (r1, r2, r3):
            total += r[rows, :].astype(f32)
        out[rows, :] = total.T.astype(bf16)


def weight_kernel(scale, pos, *refs):
    chunks, out = refs[:8], refs[8]
    zl, x = pos[2], pos[3]
    for (dz, dx), chunk in zip(PEERS, chunks):
        shard = ((zl + 2 - dz) % 2) * 4 + (x + 4 - dx) % 4
        out[pl.ds(pl.multiple_of(shard * 16, 16), 16), :] = chunk[...] * scale


def call(kernel, out_shape, in_specs, scratch=(), cost=None):
    return pl.pallas_call(
        kernel,
        out_shape=out_shape,
        in_specs=in_specs,
        out_specs=jax.tree.map(lambda _: spec(), out_shape),
        scratch_shapes=list(scratch),
        compiler_params=pltpu.CompilerParams(vmem_limit_bytes=LIMIT),
        cost_estimate=cost,
    )


def struct(*shape, dtype=bf16):
    return jax.ShapeDtypeStruct(shape, dtype)


def peer_perm(dz, dx):
    pairs = itertools.product(range(2), range(4))
    return [(z * 4 + x, ((z + dz) % 2) * 4 + (x + dx) % 4) for z, x in pairs]


def body(out_grad, preact, aggregated, weight, tiles, tile_coords, tile_count):
    smem, vmem = spec(pltpu.SMEM), spec()
    pos = jnp.stack([lax.axis_index(a) for a in ROWS + COLS]).astype(jnp.int32)
    messages = call(
        prep_kernel,
        [struct(T + 16, 2 * T)] * 8,
        [smem] + [vmem] * 4,
        [pltpu.VMEM((T, T), f32)],
    )(pos, out_grad, preact, aggregated, weight)
    own = [messages[0]]
    for (dz, dx), message in list(zip(PEERS, messages))[1:]:
        own.append(lax.ppermute(message, ("zl", "x"), peer_perm(dz, dx)))
    other = [lax.ppermute(m, "core", [(0, 1), (1, 0)]) for m in own]

    slots = tiles.shape[2]
    keep, keep_w, *sends = call(
        tile_kernel,
        [struct(1024, T, dtype=f32), struct(16, T, dtype=f32)] + [struct(1056, T)] * 3,
        [smem] * 3 + [vmem] * 16 + [spec(pl.ANY)],
        [
            pltpu.VMEM((slots, T, T), bf16),
            pltpu.VMEM((32, T, T), bf16),
            pltpu.VMEM((33, T, T), f32),
            pltpu.SemaphoreType.DMA((slots // GROUP,)),
        ],
        pl.CostEstimate(flops=slots * 2 * T**3, bytes_accessed=slots * T * T * 2, transcendentals=0),
    )(
        pos,
        tile_count.reshape(1),
        tile_coords.reshape(2, slots),
        *own,
        *other,
        tiles.reshape(slots, T, T),
    )
    turn = lambda d: [(i, (i + d) % 4) for i in range(4)]
    got = [lax.ppermute(s, "y", turn(d)) for d, s in zip((1, 2, 3), sends)]
    keep_z, keep_zw, *sends = call(
        y_kernel,
        [struct(256, T, dtype=f32), struct(16, T, dtype=f32)] + [struct(288, T)] * 3,
        [smem] + [vmem] * 5,
    )(pos, keep, keep_w, *got)
    got = [lax.ppermute(s, "zh", turn(d)) for d, s in zip((1, 2, 3), sends)]
    input_grad, chunk = call(
        z_kernel, [struct(256, T), struct(16, T, dtype=f32)], [vmem] * 5
    )(keep_z, keep_zw, *got)
    chunks = [chunk]
    for dz, dx in PEERS[1:]:
        chunks.append(lax.ppermute(chunk, ("zl", "x"), peer_perm(dz, dx)))
    devices = 1
    for a in ROWS + COLS:
        devices *= lax.axis_size(a)
    scale = 1.0 / (out_grad.shape[0] * devices) ** 0.5
    weight_grad = call(
        functools.partial(weight_kernel, scale),
        struct(T, T, dtype=f32),
        [smem] + [vmem] * 8,
    )(pos, *chunks)
    return input_grad, weight_grad


def solution(mesh):
    fine = Mesh(mesh.devices.reshape(4, 4, 2, 4, 2), ROWS + COLS)
    every = ROWS + COLS
    return jax.shard_map(
        body,
        mesh=fine,
        in_specs=(
            P(every, None),
            P(every, None),
            P(every, None),
            P(),
            P(ROWS, COLS, None, None, None),
            P(ROWS, COLS, None, None),
            P(ROWS, COLS),
        ),
        out_specs=(P(every, None), P()),
        check_vma=False,
    )
```

```python
import functools
import itertools

import jax
import jax.numpy as jnp
from jax import lax
from jax.experimental import pallas as pl
from jax.experimental.pallas import tpu as pltpu
from jax.sharding import Mesh, PartitionSpec as P

bf16 = jnp.bfloat16
f32 = jnp.float32
i32 = jnp.int32
T = 128
ROWS = ("zh", "y")
COLS = ("zl", "x", "core")
BLOCKS = 32
SLOTS = 256
PLACES = 384
PART = 32
UNROLL = 4
LIMIT = 16 * 1024 * 1024


def spec(space=pltpu.VMEM):
    return pl.BlockSpec(memory_space=space)


def split_parts(value):
    high = value.astype(bf16)
    low = (value - high.astype(f32)).astype(bf16)
    return high, low


def ring_sum(own, received):
    return (own + received[1]) + (received[0] + received[2])


def local_kernel(inputs, message):
    n = (inputs.shape[0] - T) // 3
    og, pre, agg = (inputs[pl.ds(i * n, n), :] for i in range(3))
    weight = inputs[3 * n :, :]
    grad_pre = jnp.where(pre > 0, og, jnp.zeros_like(og))
    message[0:T, :] = lax.dot_general(
        weight, grad_pre, (((1,), (1,)), ((), ())), preferred_element_type=f32
    ).astype(bf16)
    partial = lax.dot_general(
        agg, grad_pre, (((0,), (0,)), ((), ())), preferred_element_type=f32
    )
    high, low = split_parts(partial)
    message[T : 2 * T, 0:T] = high
    message[T : 2 * T, T : 2 * T] = low


def chip_kernel(pos, own, other, message):
    core = pos[4]
    message[pl.ds(pl.multiple_of(core * T, T), T), :] = own[0:T, :]
    message[pl.ds(pl.multiple_of((1 - core) * T, T), T), :] = other[0:T, :]
    sums = [m[T : 2 * T, 0:T].astype(f32) + m[T : 2 * T, T : 2 * T].astype(f32) for m in (own, other)]
    total = (sums[0] + sums[1]).astype(bf16)
    message[2 * T : 2 * T + 64, 0:T] = total[0:64, :]
    message[2 * T : 2 * T + 64, T : 2 * T] = total[64:T, :]


def order_kernel(count_ref, coords_hbm, tiles_hbm, out, tiles, coords, listed, sems):
    fetches = [
        pltpu.make_async_copy(tiles_hbm.at[part], tiles.at[part], sems.at[1 + i])
        for i, part in enumerate(pl.ds(g * PART, PART) for g in range(SLOTS // PART))
    ]
    fetch_coords = pltpu.make_async_copy(coords_hbm, coords, sems.at[0])
    fetch_coords.start()
    for fetch in fetches:
        fetch.start()
    fetch_coords.wait()
    count = count_ref[0]
    shape = (SLOTS, SLOTS)
    at_k = lax.broadcasted_iota(i32, shape, 0)
    at_j = lax.broadcasted_iota(i32, shape, 1)
    same = at_k == at_j
    row_j = jnp.broadcast_to(coords[0:1, :], shape)
    col_j = jnp.broadcast_to(coords[1:2, :], shape)

    def down(value_j):
        return jnp.sum(jnp.where(same, value_j, 0), axis=1, keepdims=True)

    def across(value_k):
        return jnp.sum(jnp.where(same, value_k, 0), axis=0, keepdims=True)

    row_k, col_k = down(row_j), down(col_j)
    live_j = at_j < count
    before = live_j & (col_j == col_k) & (at_j < at_k)
    rank_k = jnp.sum(before.astype(i32), axis=1, keepdims=True)
    opens_j = live_j & ((across(rank_k) & 1) == 0)
    pair_k = jnp.sum((opens_j & (col_j < col_k)).astype(i32), axis=1, keepdims=True) + (rank_k >> 1)
    slot_k = lax.broadcasted_iota(i32, (SLOTS, 1), 0)
    place_k = jnp.where(slot_k < count, 2 * pair_k + (rank_k & 1), -1)
    code_k = slot_k + (row_k << 8) + (col_k << 16)
    places = lax.broadcasted_iota(i32, (SLOTS, PLACES), 1)
    hit = places == place_k
    code = jnp.sum(jnp.where(hit, code_k, 0), axis=0, keepdims=True)
    found = jnp.sum(hit.astype(i32), axis=0, keepdims=True)
    code = jnp.where(found > 0, code, BLOCKS << 8)
    pairs = jnp.sum(opens_j[0:1, :].astype(i32), axis=1, keepdims=True)
    last = lax.broadcasted_iota(i32, (1, PLACES), 1) == PLACES - 1
    listed[...] = jnp.where(last, pairs, code)
    hand_over = pltpu.make_async_copy(listed, out, sems.at[0])
    hand_over.start()
    hand_over.wait()
    for fetch in fetches:
        fetch.wait()


def tile_kernel(pos, order, *refs):
    mine, got, swapped = refs[0], refs[1:5], refs[5:9]
    tiles = refs[9]
    keep, keep_w, sends = refs[10], refs[11], refs[12:15]
    grads, acc, parts = refs[15:]
    y, zl, x, core = pos[1], pos[2], pos[3], pos[4]

    arrived = [(got[k], core, k) for k in range(4)]
    arrived += [(swapped[k], 1 - core, k) for k in range(4)]
    arrived += [(mine, 0, 0)]
    for message, dz, dx in arrived:
        chip = ((zl + 2 - dz) % 2) * 4 + (x + 4 - dx) % 4
        for c in range(2):
            for h in range(2):
                grads[chip * 4 + 2 * c + h] = message[c * T : (c + 1) * T, h * T : (h + 1) * T]
        parts[chip] = message[2 * T : 2 * T + 64, :]
    grads[BLOCKS] = jnp.zeros((T, T), bf16)
    acc[...] = jnp.zeros_like(acc)
    pairs = order[0, PLACES - 1]

    @pl.loop(0, (pairs + UNROLL - 1) // UNROLL)
    def _(group):
        for u in range(UNROLL):
            pair = group * UNROLL + u
            first, second = order[0, 2 * pair], order[0, 2 * pair + 1]
            left = jnp.concatenate([grads[(first >> 8) & 63], grads[(second >> 8) & 63]], axis=1)
            right = jnp.concatenate([tiles[first & 255], tiles[second & 255]], axis=0)
            acc[first >> 16] += jnp.dot(left, right, preferred_element_type=f32)

    total = parts[0].astype(f32)
    for chip in range(1, 8):
        total += parts[chip].astype(f32)
    rounded = total.astype(bf16)
    for d in range(4):
        for zh in range(4):
            for h in range(2):
                q = (zh * 4 + (y + d) % 4) * 2 + h
                rows = pl.ds((zh * 2 + h) * T, T)
                if d == 0:
                    keep[rows, :] = acc[q]
                else:
                    sends[d - 1][rows, :] = acc[q].astype(bf16)
        if d:
            sends[d - 1][1024:1088, :] = rounded[:, 0:T]
            sends[d - 1][1088:1152, :] = rounded[:, T : 2 * T]
    keep_w[0:64, :] = rounded[:, 0:T]
    keep_w[64:T, :] = rounded[:, T : 2 * T]


def y_kernel(pos, keep, keep_w, r1, r2, r3, keep_z, keep_zw, s1, s2, s3):
    zh_me = pos[0]
    parts = [r[1024:1152, :].astype(f32) for r in (r1, r2, r3)]
    rounded = ring_sum(keep_w[...].astype(f32), parts).astype(bf16)
    keep_zw[...] = rounded
    for d, out in enumerate((keep_z, s1, s2, s3)):
        rows = pl.ds(pl.multiple_of(((zh_me + d) % 4) * 256, 256), 256)
        total = keep[rows, :]
        for r in (r1, r2, r3):
            total += r[rows, :].astype(f32)
        if d == 0:
            out[...] = total
        else:
            out[0:256, :] = total.astype(bf16)
            out[256:384, :] = rounded


def z_kernel(scale, keep_z, keep_zw, r1, r2, r3, out, weight_out):
    parts = [r[256:384, :].astype(f32) for r in (r1, r2, r3)]
    weight_out[...] = ring_sum(keep_zw[...].astype(f32), parts) * scale
    for h in range(2):
        rows = pl.ds(h * T, T)
        total = keep_z[rows, :]
        for r in (r1, r2, r3):
            total += r[rows, :].astype(f32)
        out[rows, :] = total.T.astype(bf16)


def call(kernel, out_shape, in_specs, scratch=(), cost=None, out_specs=None):
    return pl.pallas_call(
        kernel,
        out_shape=out_shape,
        in_specs=in_specs,
        out_specs=out_specs or jax.tree.map(lambda _: spec(), out_shape),
        scratch_shapes=list(scratch),
        compiler_params=pltpu.CompilerParams(vmem_limit_bytes=LIMIT),
        cost_estimate=cost,
    )


def struct(*shape, dtype=bf16):
    return jax.ShapeDtypeStruct(shape, dtype)


def chip_perm(k):
    pairs = []
    for z, x, c in itertools.product(range(2), range(4), range(2)):
        if c or k:
            pairs.append(((z * 4 + x) * 2 + c, (((z + c) % 2) * 4 + (x + k) % 4) * 2 + c))
    return pairs


def body(out_grad, preact, aggregated, weight, tiles, tile_coords, tile_count):
    smem, vmem, hbm = spec(pltpu.SMEM), spec(), spec(pltpu.HBM)
    nodes = out_grad.shape[0]
    pos = jnp.stack([lax.axis_index(a) for a in ROWS + COLS]).astype(i32)
    swap = [(0, 1), (1, 0)]
    inputs = jnp.concatenate([out_grad, preact, aggregated, weight], 0)
    local = call(local_kernel, struct(2 * T, nodes), [vmem])(inputs)
    mine = call(chip_kernel, struct(2 * T + 64, nodes), [smem, vmem, vmem])(
        pos, local, lax.ppermute(local, "core", swap)
    )
    order, held = call(
        order_kernel,
        [pltpu.SMEM((1, PLACES), i32), pltpu.VMEM((SLOTS, T, T), bf16)],
        [smem, hbm, hbm],
        [pltpu.VMEM((2, SLOTS), i32), pltpu.VMEM((1, PLACES), i32), pltpu.SemaphoreType.DMA((1 + SLOTS // PART,))],
        pl.CostEstimate(flops=0, bytes_accessed=2 * SLOTS * T * T * 2, transcendentals=0),
        (smem, vmem),
    )(
        tile_count.reshape(1),
        pltpu.with_memory_space_constraint(tile_coords.reshape(2, SLOTS), pltpu.HBM),
        pltpu.with_memory_space_constraint(tiles.reshape(SLOTS, T, T), pltpu.HBM),
    )
    got = [lax.ppermute(mine, COLS, chip_perm(k)) for k in range(4)]
    swapped = []
    for k in range(4):
        ready, _ = lax.optimization_barrier((got[k], order))
        swapped.append(lax.ppermute(ready, "core", swap))
    keep, keep_w, *sends = call(
        tile_kernel,
        [struct(1024, T, dtype=f32), struct(T, T)] + [struct(1152, T)] * 3,
        [smem] * 2 + [vmem] * 10,
        [
            pltpu.VMEM((BLOCKS + 1, T, T), bf16),
            pltpu.VMEM((BLOCKS, T, T), f32),
            pltpu.VMEM((8, 64, 2 * T), bf16),
        ],
        pl.CostEstimate(flops=SLOTS * 2 * T**3, bytes_accessed=SLOTS * T * T * 2, transcendentals=0),
    )(pos, order, mine, *got, *swapped, held)
    turn = lambda d: [(i, (i + d) % 4) for i in range(4)]
    got = [lax.ppermute(s, "y", turn(d)) for d, s in zip((1, 2, 3), sends)]
    keep_z, keep_zw, *sends = call(
        y_kernel,
        [struct(256, T, dtype=f32), struct(T, T)] + [struct(384, T)] * 3,
        [smem] + [vmem] * 5,
    )(pos, keep, keep_w, *got)
    got = [lax.ppermute(s, "zh", turn(d)) for d, s in zip((1, 2, 3), sends)]
    devices = 1
    for a in ROWS + COLS:
        devices *= lax.axis_size(a)
    scale = 1.0 / (nodes * devices) ** 0.5
    input_grad, weight_grad = call(
        functools.partial(z_kernel, scale),
        [struct(nodes, T), struct(T, T, dtype=f32)],
        [vmem] * 5,
    )(keep_z, keep_zw, *got)
    return input_grad, weight_grad


def solution(mesh):
    fine = Mesh(mesh.devices.reshape(4, 4, 2, 4, 2), ROWS + COLS)
    every = ROWS + COLS
    return jax.shard_map(
        body,
        mesh=fine,
        in_specs=(
            P(every, None),
            P(every, None),
            P(every, None),
            P(),
            P(ROWS, COLS, None, None, None),
            P(ROWS, COLS, None, None),
            P(ROWS, COLS),
        ),
        out_specs=(P(every, None), P()),
        check_vma=False,
    )
```

```python
import functools
import itertools

import jax
import jax.numpy as jnp
from jax import lax
from jax.experimental import pallas as pl
from jax.experimental.pallas import tpu as pltpu
from jax.sharding import Mesh, PartitionSpec as P

bf16 = jnp.bfloat16
f32 = jnp.float32
i32 = jnp.int32
T = 128
ROWS = ("zh", "y")
COLS = ("zl", "x", "core")
BLOCKS = 32
SLOTS = 256
PLACES = 384
PART = 32
UNROLL = 32
NOWHERE = 31
LIMIT = 16 * 1024 * 1024


def spec(space=pltpu.VMEM):
    return pl.BlockSpec(memory_space=space)


def split_parts(value):
    high = value.astype(bf16)
    low = (value - high.astype(f32)).astype(bf16)
    return high, low


def ring_sum(own, received):
    return (own + received[1]) + (received[0] + received[2])


def local_kernel(inputs, message):
    n = (inputs.shape[0] - T) // 3
    og, pre, agg = (inputs[pl.ds(i * n, n), :] for i in range(3))
    weight = inputs[3 * n :, :]
    grad_pre = jnp.where(pre > 0, og, jnp.zeros_like(og))
    message[0:T, :] = lax.dot_general(
        weight, grad_pre, (((1,), (1,)), ((), ())), preferred_element_type=f32
    ).astype(bf16)
    partial = lax.dot_general(
        agg, grad_pre, (((0,), (0,)), ((), ())), preferred_element_type=f32
    )
    high, low = split_parts(partial)
    message[T : 2 * T, 0:T] = high
    message[T : 2 * T, T : 2 * T] = low


def chip_kernel(pos, own, other, message):
    core = pos[4]
    message[pl.ds(pl.multiple_of(core * T, T), T), :] = own[0:T, :]
    message[pl.ds(pl.multiple_of((1 - core) * T, T), T), :] = other[0:T, :]
    sums = [m[T : 2 * T, 0:T].astype(f32) + m[T : 2 * T, T : 2 * T].astype(f32) for m in (own, other)]
    total = (sums[0] + sums[1]).astype(bf16)
    message[2 * T : 2 * T + 64, 0:T] = total[0:64, :]
    message[2 * T : 2 * T + 64, T : 2 * T] = total[64:T, :]


def order_kernel(pos, count_ref, coords_hbm, tiles_hbm, out, tiles, coords, listed, sems):
    fetches = [
        pltpu.make_async_copy(tiles_hbm.at[part], tiles.at[part], sems.at[1 + i])
        for i, part in enumerate(pl.ds(g * PART, PART) for g in range(SLOTS // PART))
    ]
    fetch_coords = pltpu.make_async_copy(coords_hbm, coords, sems.at[0])
    fetch_coords.start()
    for fetch in fetches:
        fetch.start()
    fetch_coords.wait()
    count, y = count_ref[0], pos[1]
    shape = (SLOTS, SLOTS)
    at_k = lax.broadcasted_iota(i32, shape, 0)
    at_j = lax.broadcasted_iota(i32, shape, 1)
    live_j = at_j < count

    def down(value_j):
        return jnp.sum(jnp.where(at_k == at_j, value_j, 0), axis=1, keepdims=True)

    col_j = coords[1:2, :]
    offset_j = (((col_j >> 1) & 3) - y) & 3
    stage_j = jnp.where(offset_j == 2, 0, jnp.where(offset_j == 0, 2, 1))
    local_j = (col_j >> 3) * 2 + (col_j & 1) + jnp.where(offset_j == 3, 8, 0)
    slot_j = lax.broadcasted_iota(i32, (1, SLOTS), 1)
    code_k = down(slot_j + (coords[0:1, :] << 8) + (local_j << 16))
    stage_k = down(stage_j)
    before = live_j & (stage_j == stage_k) & (at_j < at_k)
    place_k = jnp.sum(before.astype(i32), axis=1, keepdims=True)
    lane = lax.broadcasted_iota(i32, (1, PLACES), 1)
    base = jnp.zeros((1, 1), i32)
    numbers = jnp.zeros((1, PLACES), i32)
    for stage in range(3):
        place_k += jnp.where(stage_k == stage, base, 0)
        members = ((slot_j < count) & (stage_j == stage)).astype(i32)
        groups = (jnp.sum(members, axis=1, keepdims=True) + UNROLL - 1) // UNROLL
        numbers = jnp.where(lane == PLACES - 3 + stage, groups, numbers)
        base += groups * UNROLL
    slot_k = lax.broadcasted_iota(i32, (SLOTS, 1), 0)
    place_k = jnp.where(slot_k < count, place_k, -1)
    hit = lax.broadcasted_iota(i32, (SLOTS, PLACES), 1) == place_k
    code = jnp.sum(jnp.where(hit, code_k + 1, 0), axis=0, keepdims=True) - 1
    code = jnp.where(code < 0, NOWHERE << 16, code)
    listed[...] = jnp.where(lane >= PLACES - 3, numbers, code)
    hand_over = pltpu.make_async_copy(listed, out, sems.at[0])
    hand_over.start()
    hand_over.wait()
    for fetch in fetches:
        fetch.wait()


def multiply(stage, order, grads, tiles, acc):
    acc[...] = jnp.zeros_like(acc)
    spare = acc.shape[0] - 1
    groups = [order[0, PLACES - 3 + i] for i in range(3)]
    base = sum(groups[:stage], 0)

    @pl.loop(0, groups[stage])
    def _(group):
        for u in range(UNROLL):
            code = order[0, (base + group) * UNROLL + u]
            at = jnp.minimum(code >> 16, spare)
            acc[at] += jnp.dot(
                grads[(code >> 8) & 31], tiles[code & 255], preferred_element_type=f32
            )


def first_kernel(pos, order, *refs):
    mine, got, swapped = refs[0], refs[1:5], refs[5:9]
    tiles, grads, weight_part, send, acc, parts = refs[9:]
    zl, x, core = pos[2], pos[3], pos[4]

    arrived = [(got[k], core, k) for k in range(4)]
    arrived += [(swapped[k], 1 - core, k) for k in range(4)]
    arrived += [(mine, 0, 0)]
    for message, dz, dx in arrived:
        chip = ((zl + 2 - dz) % 2) * 4 + (x + 4 - dx) % 4
        for c in range(2):
            for h in range(2):
                grads[chip * 4 + 2 * c + h] = message[c * T : (c + 1) * T, h * T : (h + 1) * T]
        parts[chip] = message[2 * T : 2 * T + 64, :]
    total = parts[0].astype(f32)
    for chip in range(1, 8):
        total += parts[chip].astype(f32)
    rounded = total.astype(bf16)
    weight_part[0:64, :] = rounded[:, 0:T]
    weight_part[64:T, :] = rounded[:, T : 2 * T]
    multiply(0, order, grads, tiles, acc)
    for i in range(8):
        send[i * T : (i + 1) * T, :] = acc[i].astype(bf16)


def second_kernel(order, grads, tiles, send_1, send_3, acc):
    multiply(1, order, grads, tiles, acc)
    for i in range(8):
        send_1[i * T : (i + 1) * T, :] = acc[i].astype(bf16)
        send_3[i * T : (i + 1) * T, :] = acc[8 + i].astype(bf16)


def third_kernel(order, grads, tiles, keep, acc):
    multiply(2, order, grads, tiles, acc)
    for i in range(8):
        keep[i * T : (i + 1) * T, :] = acc[i]


def y_kernel(pos, keep, r1, r2, r3, keep_z, s1, s2, s3):
    zh_me = pos[0]
    for d, out in enumerate((keep_z, s1, s2, s3)):
        rows = pl.ds(pl.multiple_of(((zh_me + d) % 4) * 256, 256), 256)
        total = keep[rows, :]
        for r in (r1, r2, r3):
            total += r[rows, :].astype(f32)
        out[...] = total.astype(out.dtype)


def weight_kernel(own, r1, r2, r3, out):
    parts = [r[...].astype(f32) for r in (r1, r2, r3)]
    out[...] = ring_sum(own[...].astype(f32), parts).astype(bf16)


def z_kernel(scale, keep_z, r1, r2, r3, w0, w1, w2, w3, out, weight_out):
    parts = [w[...].astype(f32) for w in (w1, w2, w3)]
    weight_out[...] = ring_sum(w0[...].astype(f32), parts) * scale
    for h in range(2):
        rows = pl.ds(h * T, T)
        total = keep_z[rows, :]
        for r in (r1, r2, r3):
            total += r[rows, :].astype(f32)
        out[rows, :] = total.T.astype(bf16)


def call(kernel, out_shape, in_specs, scratch=(), cost=None, out_specs=None):
    return pl.pallas_call(
        kernel,
        out_shape=out_shape,
        in_specs=in_specs,
        out_specs=out_specs or jax.tree.map(lambda _: spec(), out_shape),
        scratch_shapes=list(scratch),
        compiler_params=pltpu.CompilerParams(vmem_limit_bytes=LIMIT),
        cost_estimate=cost,
    )


def struct(*shape, dtype=bf16):
    return jax.ShapeDtypeStruct(shape, dtype)


def chip_perm(k):
    pairs = []
    for z, x, c in itertools.product(range(2), range(4), range(2)):
        if c or k:
            pairs.append(((z * 4 + x) * 2 + c, (((z + c) % 2) * 4 + (x + k) % 4) * 2 + c))
    return pairs


def body(out_grad, preact, aggregated, weight, tiles, tile_coords, tile_count):
    smem, vmem, hbm = spec(pltpu.SMEM), spec(), spec(pltpu.HBM)
    nodes = out_grad.shape[0]
    pos = jnp.stack([lax.axis_index(a) for a in ROWS + COLS]).astype(i32)
    swap = [(0, 1), (1, 0)]
    inputs = jnp.concatenate([out_grad, preact, aggregated, weight], 0)
    local = call(local_kernel, struct(2 * T, nodes), [vmem])(inputs)
    mine = call(chip_kernel, struct(2 * T + 64, nodes), [smem, vmem, vmem])(
        pos, local, lax.ppermute(local, "core", swap)
    )
    order, held = call(
        order_kernel,
        [pltpu.SMEM((1, PLACES), i32), pltpu.VMEM((SLOTS, T, T), bf16)],
        [smem, smem, hbm, hbm],
        [pltpu.VMEM((2, SLOTS), i32), pltpu.VMEM((1, PLACES), i32), pltpu.SemaphoreType.DMA((1 + SLOTS // PART,))],
        pl.CostEstimate(flops=0, bytes_accessed=2 * SLOTS * T * T * 2, transcendentals=0),
        (smem, vmem),
    )(
        pos,
        tile_count.reshape(1),
        pltpu.with_memory_space_constraint(tile_coords.reshape(2, SLOTS), pltpu.HBM),
        pltpu.with_memory_space_constraint(tiles.reshape(SLOTS, T, T), pltpu.HBM),
    )
    got = [lax.ppermute(mine, COLS, chip_perm(k)) for k in range(4)]
    swapped = []
    for k in range(4):
        ready = got[k]
        if k == 3:
            ready, _ = lax.optimization_barrier((ready, order))
        swapped.append(lax.ppermute(ready, "core", swap))
    cost = lambda share: pl.CostEstimate(
        flops=share * SLOTS * 2 * T**3, bytes_accessed=share * SLOTS * T * T * 2, transcendentals=0
    )
    grads, weight_part, send_2 = call(
        first_kernel,
        [struct(BLOCKS, T, T), struct(T, T), struct(8 * T, T)],
        [smem] * 2 + [vmem] * 10,
        [pltpu.VMEM((9, T, T), f32), pltpu.VMEM((8, 64, 2 * T), bf16)],
        cost(1),
    )(pos, order, mine, *got, *swapped, held)
    send_1, send_3 = call(
        second_kernel,
        [struct(8 * T, T)] * 2,
        [smem] + [vmem] * 2,
        [pltpu.VMEM((17, T, T), f32)],
        cost(1),
    )(order, grads, held)
    keep = call(
        third_kernel,
        struct(8 * T, T, dtype=f32),
        [smem] + [vmem] * 2,
        [pltpu.VMEM((9, T, T), f32)],
        cost(1),
    )(order, grads, held)
    turn = lambda d: [(i, (i + d) % 4) for i in range(4)]
    around = lambda axis, values: [lax.ppermute(v, axis, turn(d)) for d, v in zip((1, 2, 3), values)]
    got = around("y", (send_1, send_2, send_3))
    weight_zs = around("zh", [weight_part] * 3)
    keep_z, *sends = call(
        y_kernel,
        [struct(256, T, dtype=f32)] + [struct(256, T)] * 3,
        [smem] + [vmem] * 4,
    )(pos, keep, *got)
    weight_z = call(weight_kernel, struct(T, T), [vmem] * 4)(weight_part, *weight_zs)
    weight_ys = around("y", [weight_z] * 3)
    got = around("zh", sends)
    devices = 1
    for a in ROWS + COLS:
        devices *= lax.axis_size(a)
    scale = 1.0 / (nodes * devices) ** 0.5
    input_grad, weight_grad = call(
        functools.partial(z_kernel, scale),
        [struct(nodes, T), struct(T, T, dtype=f32)],
        [vmem] * 8,
    )(keep_z, *got, weight_z, *weight_ys)
    return input_grad, weight_grad


def solution(mesh):
    fine = Mesh(mesh.devices.reshape(4, 4, 2, 4, 2), ROWS + COLS)
    every = ROWS + COLS
    return jax.shard_map(
        body,
        mesh=fine,
        in_specs=(
            P(every, None),
            P(every, None),
            P(every, None),
            P(),
            P(ROWS, COLS, None, None, None),
            P(ROWS, COLS, None, None),
            P(ROWS, COLS),
        ),
        out_specs=(P(every, None), P()),
        check_vma=False,
    )
```

```python
import functools
import itertools

import jax
import jax.numpy as jnp
from jax import lax
from jax.experimental import pallas as pl
from jax.experimental.pallas import tpu as pltpu
from jax.sharding import Mesh, PartitionSpec as P

bf16 = jnp.bfloat16
f32 = jnp.float32
i32 = jnp.int32
T = 128
ROWS = ("zh", "y")
COLS = ("zl", "x", "core")
BLOCKS = 32
SLOTS = 256
STRIDE = 320
PLACES = 1024
PART = 32
UNROLL = 32
NOWHERE = 31
LIMIT = 16 * 1024 * 1024


def spec(space=pltpu.VMEM):
    return pl.BlockSpec(memory_space=space)


def split_parts(value):
    high = value.astype(bf16)
    low = (value - high.astype(f32)).astype(bf16)
    return high, low


def ring_sum(own, received):
    return (own + received[1]) + (received[0] + received[2])


def local_kernel(inputs, message):
    n = (inputs.shape[0] - T) // 3
    og, pre, agg = (inputs[pl.ds(i * n, n), :] for i in range(3))
    weight = inputs[3 * n :, :]
    grad_pre = jnp.where(pre > 0, og, jnp.zeros_like(og))
    message[0:T, :] = lax.dot_general(
        weight, grad_pre, (((1,), (1,)), ((), ())), preferred_element_type=f32
    ).astype(bf16)
    partial = lax.dot_general(
        agg, grad_pre, (((0,), (0,)), ((), ())), preferred_element_type=f32
    )
    high, low = split_parts(partial)
    message[T : 2 * T, 0:T] = high
    message[T : 2 * T, T : 2 * T] = low


def chip_kernel(pos, own, other, message):
    core = pos[4]
    message[pl.ds(pl.multiple_of(core * T, T), T), :] = own[0:T, :]
    message[pl.ds(pl.multiple_of((1 - core) * T, T), T), :] = other[0:T, :]
    sums = [m[T : 2 * T, 0:T].astype(f32) + m[T : 2 * T, T : 2 * T].astype(f32) for m in (own, other)]
    total = (sums[0] + sums[1]).astype(bf16)
    message[2 * T : 2 * T + 64, 0:T] = total[0:64, :]
    message[2 * T : 2 * T + 64, T : 2 * T] = total[64:T, :]


def order_kernel(pos, count_ref, coords_hbm, tiles_hbm, out, tiles, coords, sems):
    fetches = [
        pltpu.make_async_copy(tiles_hbm.at[part], tiles.at[part], sems.at[1 + i])
        for i, part in enumerate(pl.ds(g * PART, PART) for g in range(SLOTS // PART))
    ]
    fetch_coords = pltpu.make_async_copy(coords_hbm, coords, sems.at[0])
    fetch_coords.start()
    for fetch in fetches:
        fetch.start()
    fetch_coords.wait()
    count, y = count_ref[0], pos[1]

    def place(k, ends):
        row, col = coords[0, k], coords[1, k]
        offset = (((col >> 1) & 3) - y) & 3
        local = (col >> 3) * 2 + (col & 1) + jnp.where(offset == 3, 8, 0)
        stage = jnp.where(offset == 2, 0, jnp.where(offset == 0, 2, 1))
        end = jnp.where(offset == 2, ends[0], jnp.where(offset == 0, ends[2], ends[1]))
        out[0, end] = k + (row << 8) + (local << 16)
        return tuple(e + (stage == i).astype(i32) for i, e in enumerate(ends))

    starts = tuple(jnp.int32(STRIDE * i) for i in range(3))
    step = 8
    whole = count // step

    def several(i, ends):
        for u in range(step):
            ends = place(i * step + u, ends)
        return ends

    ends = lax.fori_loop(0, whole, several, starts)
    ends = lax.fori_loop(whole * step, count, place, ends)
    for i in range(3):
        for u in range(UNROLL):
            out[0, ends[i] + u] = NOWHERE << 16
        out[0, STRIDE * 3 + i] = (ends[i] - STRIDE * i + UNROLL - 1) // UNROLL
    for fetch in fetches:
        fetch.wait()


def multiply(stage, order, grads, tiles, acc):
    acc[...] = jnp.zeros_like(acc)
    spare = acc.shape[0] - 1

    @pl.loop(0, order[0, STRIDE * 3 + stage])
    def _(group):
        for u in range(UNROLL):
            code = order[0, STRIDE * stage + group * UNROLL + u]
            at = jnp.minimum(code >> 16, spare)
            acc[at] += jnp.dot(
                grads[(code >> 8) & 31], tiles[code & 255], preferred_element_type=f32
            )


def first_kernel(pos, order, *refs):
    mine, got, swapped = refs[0], refs[1:5], refs[5:9]
    tiles, grads, weight_part, send, acc, parts = refs[9:]
    zl, x, core = pos[2], pos[3], pos[4]

    arrived = [(got[k], core, k) for k in range(4)]
    arrived += [(swapped[k], 1 - core, k) for k in range(4)]
    arrived += [(mine, 0, 0)]
    for message, dz, dx in arrived:
        chip = ((zl + 2 - dz) % 2) * 4 + (x + 4 - dx) % 4
        for c in range(2):
            for h in range(2):
                grads[chip * 4 + 2 * c + h] = message[c * T : (c + 1) * T, h * T : (h + 1) * T]
        parts[chip] = message[2 * T : 2 * T + 64, :]
    total = parts[0].astype(f32)
    for chip in range(1, 8):
        total += parts[chip].astype(f32)
    rounded = total.astype(bf16)
    weight_part[0:64, :] = rounded[:, 0:T]
    weight_part[64:T, :] = rounded[:, T : 2 * T]
    multiply(0, order, grads, tiles, acc)
    for i in range(8):
        send[i * T : (i + 1) * T, :] = acc[i].astype(bf16)
    send[8 * T : 9 * T, :] = weight_part[...]


def second_kernel(order, grads, weight_part, tiles, send_1, send_3, acc):
    multiply(1, order, grads, tiles, acc)
    for send in (send_1, send_3):
        send[8 * T : 9 * T, :] = weight_part[...]
    for i in range(8):
        send_1[i * T : (i + 1) * T, :] = acc[i].astype(bf16)
        send_3[i * T : (i + 1) * T, :] = acc[8 + i].astype(bf16)


def third_kernel(order, grads, tiles, keep, acc):
    multiply(2, order, grads, tiles, acc)
    for i in range(8):
        keep[i * T : (i + 1) * T, :] = acc[i]


def y_kernel(pos, keep, weight_part, r1, r2, r3, keep_z, keep_zw, s1, s2, s3):
    zh_me = pos[0]
    parts = [r[8 * T : 9 * T, :].astype(f32) for r in (r1, r2, r3)]
    rounded = ring_sum(weight_part[...].astype(f32), parts).astype(bf16)
    keep_zw[...] = rounded
    for d, out in enumerate((keep_z, s1, s2, s3)):
        rows = pl.ds(pl.multiple_of(((zh_me + d) % 4) * 256, 256), 256)
        total = keep[rows, :]
        for r in (r1, r2, r3):
            total += r[rows, :].astype(f32)
        out[0:256, :] = total.astype(out.dtype)
        if d:
            out[256:384, :] = rounded


def z_kernel(scale, keep_z, keep_zw, r1, r2, r3, out, weight_out):
    parts = [r[256:384, :].astype(f32) for r in (r1, r2, r3)]
    weight_out[...] = ring_sum(keep_zw[...].astype(f32), parts) * scale
    for h in range(2):
        rows = pl.ds(h * T, T)
        total = keep_z[rows, :]
        for r in (r1, r2, r3):
            total += r[rows, :].astype(f32)
        out[rows, :] = total.T.astype(bf16)


def call(kernel, out_shape, in_specs, scratch=(), cost=None, out_specs=None):
    return pl.pallas_call(
        kernel,
        out_shape=out_shape,
        in_specs=in_specs,
        out_specs=out_specs or jax.tree.map(lambda _: spec(), out_shape),
        scratch_shapes=list(scratch),
        compiler_params=pltpu.CompilerParams(vmem_limit_bytes=LIMIT),
        cost_estimate=cost,
    )


def struct(*shape, dtype=bf16):
    return jax.ShapeDtypeStruct(shape, dtype)


def chip_perm(k):
    pairs = []
    for z, x, c in itertools.product(range(2), range(4), range(2)):
        if c or k:
            pairs.append(((z * 4 + x) * 2 + c, (((z + c) % 2) * 4 + (x + k) % 4) * 2 + c))
    return pairs


def body(out_grad, preact, aggregated, weight, tiles, tile_coords, tile_count):
    smem, vmem, hbm = spec(pltpu.SMEM), spec(), spec(pltpu.HBM)
    nodes = out_grad.shape[0]
    pos = jnp.stack([lax.axis_index(a) for a in ROWS + COLS]).astype(i32)
    swap = [(0, 1), (1, 0)]
    inputs = jnp.concatenate([out_grad, preact, aggregated, weight], 0)
    local = call(local_kernel, struct(2 * T, nodes), [vmem])(inputs)
    mine = call(chip_kernel, struct(2 * T + 64, nodes), [smem, vmem, vmem])(
        pos, local, lax.ppermute(local, "core", swap)
    )
    order, held = call(
        order_kernel,
        [pltpu.SMEM((1, PLACES), i32), pltpu.VMEM((SLOTS, T, T), bf16)],
        [smem, smem, hbm, hbm],
        [pltpu.SMEM((2, SLOTS), i32), pltpu.SemaphoreType.DMA((1 + SLOTS // PART,))],
        pl.CostEstimate(flops=0, bytes_accessed=2 * SLOTS * T * T * 2, transcendentals=0),
        (smem, vmem),
    )(
        pos,
        tile_count.reshape(1),
        pltpu.with_memory_space_constraint(tile_coords.reshape(2, SLOTS), pltpu.HBM),
        pltpu.with_memory_space_constraint(tiles.reshape(SLOTS, T, T), pltpu.HBM),
    )
    got = [lax.ppermute(mine, COLS, chip_perm(k)) for k in range(4)]
    swapped = []
    for k in range(4):
        ready = got[k]
        if k == 3:
            ready, _ = lax.optimization_barrier((ready, order))
        swapped.append(lax.ppermute(ready, "core", swap))
    cost = lambda share: pl.CostEstimate(
        flops=share * SLOTS * 2 * T**3, bytes_accessed=share * SLOTS * T * T * 2, transcendentals=0
    )
    grads, weight_part, send_2 = call(
        first_kernel,
        [struct(BLOCKS, T, T), struct(T, T), struct(9 * T, T)],
        [smem] * 2 + [vmem] * 10,
        [pltpu.VMEM((9, T, T), f32), pltpu.VMEM((8, 64, 2 * T), bf16)],
        cost(1),
    )(pos, order, mine, *got, *swapped, held)
    send_1, send_3 = call(
        second_kernel,
        [struct(9 * T, T)] * 2,
        [smem] + [vmem] * 3,
        [pltpu.VMEM((17, T, T), f32)],
        cost(1),
    )(order, grads, weight_part, held)
    keep = call(
        third_kernel,
        struct(8 * T, T, dtype=f32),
        [smem] + [vmem] * 2,
        [pltpu.VMEM((9, T, T), f32)],
        cost(1),
    )(order, grads, held)
    turn = lambda d: [(i, (i + d) % 4) for i in range(4)]
    around = lambda axis, values: [lax.ppermute(v, axis, turn(d)) for d, v in zip((1, 2, 3), values)]
    got = around("y", (send_1, send_2, send_3))
    keep_z, keep_zw, *sends = call(
        y_kernel,
        [struct(256, T, dtype=f32), struct(T, T)] + [struct(384, T)] * 3,
        [smem] + [vmem] * 5,
    )(pos, keep, weight_part, *got)
    got = around("zh", sends)
    devices = 1
    for a in ROWS + COLS:
        devices *= lax.axis_size(a)
    scale = 1.0 / (nodes * devices) ** 0.5
    input_grad, weight_grad = call(
        functools.partial(z_kernel, scale),
        [struct(nodes, T), struct(T, T, dtype=f32)],
        [vmem] * 5,
    )(keep_z, keep_zw, *got)
    return input_grad, weight_grad


def solution(mesh):
    fine = Mesh(mesh.devices.reshape(4, 4, 2, 4, 2), ROWS + COLS)
    every = ROWS + COLS
    return jax.shard_map(
        body,
        mesh=fine,
        in_specs=(
            P(every, None),
            P(every, None),
            P(every, None),
            P(),
            P(ROWS, COLS, None, None, None),
            P(ROWS, COLS, None, None),
            P(ROWS, COLS),
        ),
        out_specs=(P(every, None), P()),
        check_vma=False,
    )
```

```python
import functools

import jax
import jax.numpy as jnp
from jax import lax
from jax.experimental import pallas as pl
from jax.experimental.pallas import tpu as pltpu
from jax.sharding import Mesh, PartitionSpec as P

bf16 = jnp.bfloat16
f32 = jnp.float32
i32 = jnp.int32
T = 128
ROWS = ("zh", "y")
COLS = ("zl", "x", "core")
BLOCKS = 32
SLOTS = 256
STRIDE = 320
PLACES = 1024
PART = 16
UNROLL = 32
NOWHERE = 31
LIMIT = 16 * 1024 * 1024


def spec(space=pltpu.VMEM):
    return pl.BlockSpec(memory_space=space)


def ring_sum(own, received):
    return (own + received[1]) + (received[0] + received[2])


def local_kernel(inputs, message):
    n = (inputs.shape[0] - T) // 3
    og, pre, agg = (inputs[pl.ds(i * n, n), :] for i in range(3))
    weight = inputs[3 * n :, :]
    grad_pre = jnp.where(pre > 0, og, jnp.zeros_like(og))
    message[0:T, :] = lax.dot_general(
        weight, grad_pre, (((1,), (1,)), ((), ())), preferred_element_type=f32
    ).astype(bf16)
    partial = lax.dot_general(
        agg, grad_pre, (((0,), (0,)), ((), ())), preferred_element_type=f32
    ).astype(bf16)
    message[T : T + 64, 0:T] = partial[0:64, :]
    message[T : T + 64, T : 2 * T] = partial[64:T, :]


def chip_kernel(pos, own, crossed, other, message):
    def make(first, second):
        message[0:T, :] = first[0:T, :]
        message[T : 2 * T, :] = second[0:T, :]
        total = first[T : T + 64, :].astype(f32) + second[T : T + 64, :].astype(f32)
        message[2 * T : 2 * T + 64, :] = total.astype(bf16)

    @pl.when(pos[4] == 0)
    def _():
        make(own, crossed)

    @pl.when(pos[4] == 1)
    def _():
        make(crossed, other)


def order_kernel(pos, count_ref, coords_hbm, tiles_hbm, out, tiles, coords, sems):
    fetches = [
        pltpu.make_async_copy(tiles_hbm.at[part], tiles.at[part], sems.at[1 + i])
        for i, part in enumerate(pl.ds(g * PART, PART) for g in range(SLOTS // PART))
    ]
    fetch_coords = pltpu.make_async_copy(coords_hbm, coords, sems.at[0])
    fetch_coords.start()
    count, y = count_ref[0], pos[1]
    for g, fetch in enumerate(fetches):
        pl.when(g * PART < count)(fetch.start)
    fetch_coords.wait()
    turn = 1 - 2 * pos[4]

    def place(k, ends):
        row, col = coords[0, k], coords[1, k]
        offset = ((((col >> 1) & 3) - y) * turn) & 3
        local = (col >> 3) * 2 + (col & 1) + jnp.where(offset == 3, 8, 0)
        stage = jnp.where(offset == 2, 0, jnp.where(offset == 0, 2, 1))
        end = jnp.where(offset == 2, ends[0], jnp.where(offset == 0, ends[2], ends[1]))
        out[0, end] = k + (row << 8) + (local << 16)
        return tuple(e + (stage == i).astype(i32) for i, e in enumerate(ends))

    starts = tuple(jnp.int32(STRIDE * i) for i in range(3))
    step = 8
    whole = count // step

    def several(i, ends):
        for u in range(step):
            ends = place(i * step + u, ends)
        return ends

    ends = lax.fori_loop(0, whole, several, starts)
    ends = lax.fori_loop(whole * step, count, place, ends)
    for i in range(3):
        for u in range(UNROLL):
            out[0, ends[i] + u] = NOWHERE << 16
        out[0, STRIDE * 3 + i] = (ends[i] - STRIDE * i + UNROLL - 1) // UNROLL
    for g, fetch in enumerate(fetches):
        pl.when(g * PART < count)(fetch.wait)


def multiply(stage, order, grads, tiles, acc):
    acc[...] = jnp.zeros_like(acc)
    spare = acc.shape[0] - 1

    @pl.loop(0, order[0, STRIDE * 3 + stage])
    def _(group):
        for u in range(UNROLL):
            code = order[0, STRIDE * stage + group * UNROLL + u]
            at = jnp.minimum(code >> 16, spare)
            acc[at] += jnp.dot(
                grads[(code >> 8) & 31], tiles[code & 255], preferred_element_type=f32
            )


def first_kernel(pos, order, *refs):
    got, swapped = refs[0:4], refs[4:8]
    tiles, grads, weight_part, send, acc, parts = refs[8:]
    zl, x, core = pos[2], pos[3], pos[4]

    for messages, side in ((got, core), (swapped, 1 - core)):
        for k, message in enumerate(messages):
            chip = ((zl + side) & 1) * 4 + ((x - k * (1 - 2 * side)) & 3)
            for c in range(2):
                for h in range(2):
                    rows, columns = slice(c * T, (c + 1) * T), slice(h * T, (h + 1) * T)
                    grads[chip * 4 + 2 * c + h] = message[rows, columns]
            parts[chip] = message[2 * T : 2 * T + 64, :]
    total = parts[0].astype(f32)
    for chip in range(1, 8):
        total += parts[chip].astype(f32)
    rounded = total.astype(bf16)
    weight_part[0:64, :] = rounded[:, 0:T]
    weight_part[64:T, :] = rounded[:, T : 2 * T]
    multiply(0, order, grads, tiles, acc)
    for i in range(8):
        send[i * T : (i + 1) * T, :] = acc[i].astype(bf16)
    send[8 * T : 9 * T, :] = weight_part[...]


def second_kernel(order, grads, weight_part, tiles, send_1, send_3, acc):
    multiply(1, order, grads, tiles, acc)
    for send in (send_1, send_3):
        send[8 * T : 9 * T, :] = weight_part[...]
    for i in range(8):
        send_1[i * T : (i + 1) * T, :] = acc[i].astype(bf16)
        send_3[i * T : (i + 1) * T, :] = acc[8 + i].astype(bf16)


def third_kernel(order, grads, tiles, keep, acc):
    multiply(2, order, grads, tiles, acc)
    for i in range(8):
        keep[i * T : (i + 1) * T, :] = acc[i]


def y_kernel(pos, keep, weight_part, r1, r2, r3, keep_z, keep_zw, s1, s2, s3):
    zh_me, turn = pos[0], 1 - 2 * pos[4]
    parts = [r[8 * T : 9 * T, :].astype(f32) for r in (r1, r2, r3)]
    rounded = ring_sum(weight_part[...].astype(f32), parts).astype(bf16)
    keep_zw[...] = rounded
    for d, out in enumerate((keep_z, s1, s2, s3)):
        rows = pl.ds(pl.multiple_of(((zh_me + d * turn) & 3) * 256, 256), 256)
        total = keep[rows, :]
        for r in (r1, r2, r3):
            total += r[rows, :].astype(f32)
        out[0:256, :] = total.astype(out.dtype)
        if d:
            out[256:384, :] = rounded


def z_kernel(scale, keep_z, keep_zw, r1, r2, r3, out, weight_out):
    parts = [r[256:384, :].astype(f32) for r in (r1, r2, r3)]
    weight_out[...] = ring_sum(keep_zw[...].astype(f32), parts) * scale
    for h in range(2):
        rows = pl.ds(h * T, T)
        total = keep_z[rows, :]
        for r in (r1, r2, r3):
            total += r[rows, :].astype(f32)
        out[rows, :] = total.T.astype(bf16)


def call(kernel, out_shape, in_specs, scratch=(), cost=None, out_specs=None):
    return pl.pallas_call(
        kernel,
        out_shape=out_shape,
        in_specs=in_specs,
        out_specs=out_specs or jax.tree.map(lambda _: spec(), out_shape),
        scratch_shapes=list(scratch),
        compiler_params=pltpu.CompilerParams(vmem_limit_bytes=LIMIT),
        cost_estimate=cost,
    )


def struct(*shape, dtype=bf16):
    return jax.ShapeDtypeStruct(shape, dtype)


def around(axis, values):
    out = []
    for d, value in enumerate(values, 1):
        pairs = [(i * 2, ((i + d) % 4) * 2) for i in range(4)]
        pairs += [(i * 2 + 1, ((i - d) % 4) * 2 + 1) for i in range(4)]
        out.append(lax.ppermute(value, (axis, "core"), pairs))
    return out


def body(out_grad, preact, aggregated, weight, tiles, tile_coords, tile_count):
    smem, vmem, hbm = spec(pltpu.SMEM), spec(), spec(pltpu.HBM)
    nodes = out_grad.shape[0]
    pos = jnp.stack([lax.axis_index(a) for a in ROWS + COLS]).astype(i32)
    inputs = jnp.concatenate([out_grad, preact, aggregated, weight], 0)
    local = call(local_kernel, struct(T + 64, nodes), [vmem])(inputs)
    crossed = lax.ppermute(local, ("zl", "core"), [(0, 3), (1, 0), (2, 1), (3, 2)])
    other = lax.ppermute(local, ("zl", "core"), [(1, 3), (3, 1)])
    chip = call(chip_kernel, struct(2 * T + 64, nodes), [smem] + [vmem] * 3)(
        pos, local, crossed, other
    )
    order, held = call(
        order_kernel,
        [pltpu.SMEM((1, PLACES), i32), pltpu.VMEM((SLOTS, T, T), bf16)],
        [smem, smem, hbm, hbm],
        [pltpu.SMEM((2, SLOTS), i32), pltpu.SemaphoreType.DMA((1 + SLOTS // PART,))],
        pl.CostEstimate(flops=0, bytes_accessed=2 * SLOTS * T * T * 2, transcendentals=0),
        (smem, vmem),
    )(
        pos,
        tile_count.reshape(1),
        pltpu.with_memory_space_constraint(tile_coords.reshape(2, SLOTS), pltpu.HBM),
        pltpu.with_memory_space_constraint(tiles.reshape(SLOTS, T, T), pltpu.HBM),
    )
    got = [chip] + around("x", [chip] * 3)
    swapped = []
    for k in range(4):
        ready = got[k]
        if k == 1:
            ready, _ = lax.optimization_barrier((ready, order))
        swapped.append(lax.ppermute(ready, "core", [(0, 1), (1, 0)]))
    cost = lambda share: pl.CostEstimate(
        flops=share * SLOTS * 2 * T**3, bytes_accessed=share * SLOTS * T * T * 2, transcendentals=0
    )
    grads, weight_part, send_2 = call(
        first_kernel,
        [struct(BLOCKS, T, T), struct(T, T), struct(9 * T, T)],
        [smem] * 2 + [vmem] * 9,
        [pltpu.VMEM((9, T, T), f32), pltpu.VMEM((8, 64, 2 * T), bf16)],
        cost(1),
    )(pos, order, *got, *swapped, held)
    send_1, send_3 = call(
        second_kernel,
        [struct(9 * T, T)] * 2,
        [smem] + [vmem] * 3,
        [pltpu.VMEM((17, T, T), f32)],
        cost(1),
    )(order, grads, weight_part, held)
    keep = call(
        third_kernel,
        struct(8 * T, T, dtype=f32),
        [smem] + [vmem] * 2,
        [pltpu.VMEM((9, T, T), f32)],
        cost(1),
    )(order, grads, held)
    got = around("y", (send_1, send_2, send_3))
    keep_z, keep_zw, *sends = call(
        y_kernel,
        [struct(256, T, dtype=f32), struct(T, T)] + [struct(384, T)] * 3,
        [smem] + [vmem] * 5,
    )(pos, keep, weight_part, *got)
    got = around("zh", sends)
    devices = 1
    for a in ROWS + COLS:
        devices *= lax.axis_size(a)
    scale = 1.0 / (nodes * devices) ** 0.5
    input_grad, weight_grad = call(
        functools.partial(z_kernel, scale),
        [struct(nodes, T), struct(T, T, dtype=f32)],
        [vmem] * 5,
    )(keep_z, keep_zw, *got)
    return input_grad, weight_grad


def solution(mesh):
    fine = Mesh(mesh.devices.reshape(4, 4, 2, 4, 2), ROWS + COLS)
    every = ROWS + COLS
    return jax.shard_map(
        body,
        mesh=fine,
        in_specs=(
            P(every, None),
            P(every, None),
            P(every, None),
            P(),
            P(ROWS, COLS, None, None, None),
            P(ROWS, COLS, None, None),
            P(ROWS, COLS),
        ),
        out_specs=(P(every, None), P()),
        check_vma=False,
    )
```

```python
import functools

import jax
import jax.numpy as jnp
from jax import lax
from jax.experimental import pallas as pl
from jax.experimental.pallas import tpu as pltpu
from jax.sharding import Mesh, PartitionSpec as P

bf16 = jnp.bfloat16
f32 = jnp.float32
i32 = jnp.int32
T = 128
ROWS = ("zh", "y")
COLS = ("zl", "x", "core")
BLOCKS = 32
SLOTS = 256
STRIDE = 320
PLACES = 1024
PART = 16
UNROLL = 32
NOWHERE = 31
LIMIT = 16 * 1024 * 1024


def spec(space=pltpu.VMEM):
    return pl.BlockSpec(memory_space=space)


def split_parts(value):
    high = value.astype(bf16)
    low = (value - high.astype(f32)).astype(bf16)
    return high, low


def ring_sum(own, received):
    return (own + received[1]) + (received[0] + received[2])


def local_kernel(inputs, message):
    n = (inputs.shape[0] - T) // 3
    og, pre, agg = (inputs[pl.ds(i * n, n), :] for i in range(3))
    weight = inputs[3 * n :, :]
    grad_pre = jnp.where(pre > 0, og, jnp.zeros_like(og))
    message[0:T, :] = lax.dot_general(
        weight, grad_pre, (((1,), (1,)), ((), ())), preferred_element_type=f32
    ).astype(bf16)
    partial = lax.dot_general(
        agg, grad_pre, (((0,), (0,)), ((), ())), preferred_element_type=f32
    )
    high, low = split_parts(partial)
    message[T : 2 * T, 0:T] = high
    message[T : 2 * T, T : 2 * T] = low


def chip_kernel(pos, own, other, message):
    core = pos[4]
    message[pl.ds(pl.multiple_of(core * T, T), T), :] = own[0:T, :]
    message[pl.ds(pl.multiple_of((1 - core) * T, T), T), :] = other[0:T, :]
    sums = [m[T : 2 * T, 0:T].astype(f32) + m[T : 2 * T, T : 2 * T].astype(f32) for m in (own, other)]
    total = (sums[0] + sums[1]).astype(bf16)
    message[2 * T : 2 * T + 64, 0:T] = total[0:64, :]
    message[2 * T : 2 * T + 64, T : 2 * T] = total[64:T, :]


def order_kernel(pos, count_ref, coords_hbm, tiles_hbm, out, tiles, coords, sems):
    fetches = [
        pltpu.make_async_copy(tiles_hbm.at[part], tiles.at[part], sems.at[1 + i])
        for i, part in enumerate(pl.ds(g * PART, PART) for g in range(SLOTS // PART))
    ]
    fetch_coords = pltpu.make_async_copy(coords_hbm, coords, sems.at[0])
    fetch_coords.start()
    count, y = count_ref[0], pos[1]
    for g, fetch in enumerate(fetches):
        pl.when(g * PART < count)(fetch.start)
    fetch_coords.wait()
    zh, turn = pos[0], 1 - 2 * pos[4]

    def place(k, ends):
        row, col = coords[0, k], coords[1, k]
        offset = ((((col >> 1) & 3) - y) * turn) & 3
        z_place = (((col >> 3) - zh) * turn + 2) & 3
        local = z_place * 2 + (col & 1) + jnp.where(offset == 3, 8, 0)
        stage = jnp.where(offset == 2, 0, jnp.where(offset == 0, 2, 1))
        end = jnp.where(offset == 2, ends[0], jnp.where(offset == 0, ends[2], ends[1]))
        out[0, end] = k + (row << 8) + (local << 16)
        return tuple(e + (stage == i).astype(i32) for i, e in enumerate(ends))

    starts = tuple(jnp.int32(STRIDE * i) for i in range(3))
    step = 8
    whole = count // step

    def several(i, ends):
        for u in range(step):
            ends = place(i * step + u, ends)
        return ends

    ends = lax.fori_loop(0, whole, several, starts)
    ends = lax.fori_loop(whole * step, count, place, ends)
    for i in range(3):
        for u in range(UNROLL):
            out[0, ends[i] + u] = NOWHERE << 16
        out[0, STRIDE * 3 + i] = (ends[i] - STRIDE * i + UNROLL - 1) // UNROLL
    for g, fetch in enumerate(fetches):
        pl.when(g * PART < count)(fetch.wait)


def multiply(stage, order, grads, tiles, acc):
    acc[...] = jnp.zeros_like(acc)
    spare = acc.shape[0] - 1

    @pl.loop(0, order[0, STRIDE * 3 + stage])
    def _(group):
        for u in range(UNROLL):
            code = order[0, STRIDE * stage + group * UNROLL + u]
            at = jnp.minimum(code >> 16, spare)
            acc[at] += jnp.dot(
                grads[(code >> 8) & 31], tiles[code & 255], preferred_element_type=f32
            )


def first_kernel(pos, order, *refs):
    mine, got, swapped = refs[0], refs[1:5], refs[5:9]
    tiles, grads, weight_part, send, acc, parts = refs[9:]
    zl, x, core = pos[2], pos[3], pos[4]

    arrived = [(got[k], core, k) for k in range(4)]
    arrived += [(swapped[k], 1 - core, k) for k in range(4)]
    arrived += [(mine, 0, 0)]
    for message, side, k in arrived:
        chip = ((zl + side) & 1) * 4 + ((x - k * (1 - 2 * side)) & 3)
        for c in range(2):
            for h in range(2):
                grads[chip * 4 + 2 * c + h] = message[c * T : (c + 1) * T, h * T : (h + 1) * T]
        parts[chip] = message[2 * T : 2 * T + 64, :]
    total = parts[0].astype(f32)
    for chip in range(1, 8):
        total += parts[chip].astype(f32)
    rounded = total.astype(bf16)
    weight_part[0:64, :] = rounded[:, 0:T]
    weight_part[64:T, :] = rounded[:, T : 2 * T]
    multiply(0, order, grads, tiles, acc)
    for i in range(8):
        send[i * T : (i + 1) * T, :] = acc[i].astype(bf16)
    send[8 * T : 9 * T, :] = weight_part[...]


def second_kernel(order, grads, weight_part, tiles, early_1, late_1, early_3, late_3, acc):
    multiply(1, order, grads, tiles, acc)
    for first, early, late in ((0, early_1, late_1), (8, early_3, late_3)):
        for i in range(2):
            early[i * T : (i + 1) * T, :] = acc[first + i].astype(bf16)
        early[2 * T : 3 * T, :] = weight_part[...]
        for i in range(6):
            late[i * T : (i + 1) * T, :] = acc[first + 2 + i].astype(bf16)


def third_kernel(order, grads, tiles, after, early, late, acc):
    del after
    multiply(2, order, grads, tiles, acc)
    for i in range(2):
        early[i * T : (i + 1) * T, :] = acc[i]
    for i in range(6):
        late[i * T : (i + 1) * T, :] = acc[2 + i]


def early_kernel(own, weight_part, r1, r2, r3, send, weight_y):
    parts = [r1[2 * T : 3 * T, :], r2[8 * T : 9 * T, :], r3[2 * T : 3 * T, :]]
    rounded = ring_sum(weight_part[...].astype(f32), [p.astype(f32) for p in parts]).astype(bf16)
    weight_y[...] = rounded
    total = own[...]
    for r in (r1, r2, r3):
        total += r[0 : 2 * T, :].astype(f32)
    send[0 : 2 * T, :] = total.astype(bf16)
    send[2 * T : 3 * T, :] = rounded


def late_kernel(own, weight_y, r1, r2, r3, send_3, keep, send_1):
    for i, out in enumerate((send_3, keep, send_1)):
        rows = pl.ds(i * 2 * T, 2 * T)
        total = own[rows, :] + r2[(i + 1) * 2 * T : (i + 2) * 2 * T, :].astype(f32)
        for r in (r1, r3):
            total += r[rows, :].astype(f32)
        out[0 : 2 * T, :] = total.astype(out.dtype)
    for out in (send_3, send_1):
        out[2 * T : 3 * T, :] = weight_y[...]


def z_kernel(scale, keep, weight_y, r1, r2, r3, out, weight_out):
    parts = [r[2 * T : 3 * T, :].astype(f32) for r in (r1, r2, r3)]
    weight_out[...] = ring_sum(weight_y[...].astype(f32), parts) * scale
    for h in range(2):
        rows = pl.ds(h * T, T)
        total = keep[rows, :]
        for r in (r1, r2, r3):
            total += r[rows, :].astype(f32)
        out[rows, :] = total.T.astype(bf16)


def call(kernel, out_shape, in_specs, scratch=(), cost=None, out_specs=None):
    return pl.pallas_call(
        kernel,
        out_shape=out_shape,
        in_specs=in_specs,
        out_specs=out_specs or jax.tree.map(lambda _: spec(), out_shape),
        scratch_shapes=list(scratch),
        compiler_params=pltpu.CompilerParams(vmem_limit_bytes=LIMIT),
        cost_estimate=cost,
    )


def struct(*shape, dtype=bf16):
    return jax.ShapeDtypeStruct(shape, dtype)


def around(axis, value, d):
    pairs = [(i * 2, ((i + d) % 4) * 2) for i in range(4)]
    pairs += [(i * 2 + 1, ((i - d) % 4) * 2 + 1) for i in range(4)]
    return lax.ppermute(value, (axis, "core"), pairs)


def chip_perm(k):
    pairs = []
    for z in range(2):
        for x in range(4):
            at = (z * 4 + x) * 2
            if k:
                pairs.append((at, (z * 4 + (x + k) % 4) * 2))
            pairs.append((at + 1, ((1 - z) * 4 + (x - k) % 4) * 2 + 1))
    return pairs


def body(out_grad, preact, aggregated, weight, tiles, tile_coords, tile_count):
    smem, vmem, hbm = spec(pltpu.SMEM), spec(), spec(pltpu.HBM)
    nodes = out_grad.shape[0]
    pos = jnp.stack([lax.axis_index(a) for a in ROWS + COLS]).astype(i32)
    inputs = jnp.concatenate([out_grad, preact, aggregated, weight], 0)
    swap = [(0, 1), (1, 0)]
    local = call(local_kernel, struct(2 * T, nodes), [vmem])(inputs)
    mine = call(chip_kernel, struct(2 * T + 64, nodes), [smem, vmem, vmem])(
        pos, local, lax.ppermute(local, "core", swap)
    )
    order, held = call(
        order_kernel,
        [pltpu.SMEM((1, PLACES), i32), pltpu.VMEM((SLOTS, T, T), bf16)],
        [smem, smem, hbm, hbm],
        [pltpu.SMEM((2, SLOTS), i32), pltpu.SemaphoreType.DMA((1 + SLOTS // PART,))],
        pl.CostEstimate(flops=0, bytes_accessed=2 * SLOTS * T * T * 2, transcendentals=0),
        (smem, vmem),
    )(
        pos,
        tile_count.reshape(1),
        pltpu.with_memory_space_constraint(tile_coords.reshape(2, SLOTS), pltpu.HBM),
        pltpu.with_memory_space_constraint(tiles.reshape(SLOTS, T, T), pltpu.HBM),
    )
    got = [lax.ppermute(mine, COLS, chip_perm(k)) for k in range(4)]
    swapped = []
    for k in range(4):
        ready = got[k]
        if k == 3:
            ready, _ = lax.optimization_barrier((ready, order))
        swapped.append(lax.ppermute(ready, "core", swap))
    cost = lambda share: pl.CostEstimate(
        flops=share * SLOTS * 2 * T**3, bytes_accessed=share * SLOTS * T * T * 2, transcendentals=0
    )
    early, late = struct(3 * T, T), struct(6 * T, T)
    grads, weight_part, send_2 = call(
        first_kernel,
        [struct(BLOCKS, T, T), struct(T, T), struct(9 * T, T)],
        [smem] * 2 + [vmem] * 10,
        [pltpu.VMEM((9, T, T), f32), pltpu.VMEM((8, 64, 2 * T), bf16)],
        cost(1),
    )(pos, order, mine, *got, *swapped, held)
    early_1, late_1, early_3, late_3 = call(
        second_kernel,
        [early, late] * 2,
        [smem] + [vmem] * 3,
        [pltpu.VMEM((17, T, T), f32)],
        cost(1),
    )(order, grads, weight_part, held)
    got_2 = around("y", send_2, 2)
    own_early, own_late = call(
        third_kernel,
        [struct(2 * T, T, dtype=f32), struct(6 * T, T, dtype=f32)],
        [smem] + [vmem] * 2 + [spec(pl.ANY)],
        [pltpu.VMEM((9, T, T), f32)],
        cost(1),
    )(order, grads, held, got_2)
    got_early = [around("y", early_1, 1), got_2, around("y", early_3, 3)]
    late_1, _ = lax.optimization_barrier((late_1, got_early[0]))
    late_3, _ = lax.optimization_barrier((late_3, got_early[2]))
    got_late = [around("y", late_1, 1), got_2, around("y", late_3, 3)]
    send_2, weight_y = call(early_kernel, [early, struct(T, T)], [vmem] * 5)(
        own_early, weight_part, *got_early
    )
    z_2 = around("zh", send_2, 2)
    send_3, keep, send_1 = call(
        late_kernel, [early, struct(2 * T, T, dtype=f32), early], [vmem] * 5
    )(own_late, weight_y, *got_late)
    z_1, z_3 = around("zh", send_1, 1), around("zh", send_3, 3)
    devices = 1
    for a in ROWS + COLS:
        devices *= lax.axis_size(a)
    scale = 1.0 / (nodes * devices) ** 0.5
    input_grad, weight_grad = call(
        functools.partial(z_kernel, scale),
        [struct(nodes, T), struct(T, T, dtype=f32)],
        [vmem] * 5,
    )(keep, weight_y, z_1, z_2, z_3)
    return input_grad, weight_grad


def solution(mesh):
    fine = Mesh(mesh.devices.reshape(4, 4, 2, 4, 2), ROWS + COLS)
    every = ROWS + COLS
    return jax.shard_map(
        body,
        mesh=fine,
        in_specs=(
            P(every, None),
            P(every, None),
            P(every, None),
            P(),
            P(ROWS, COLS, None, None, None),
            P(ROWS, COLS, None, None),
            P(ROWS, COLS),
        ),
        out_specs=(P(every, None), P()),
        check_vma=False,
    )
```

```python
import functools

import jax
import jax.numpy as jnp
from jax import lax
from jax.experimental import pallas as pl
from jax.experimental.pallas import tpu as pltpu
from jax.sharding import Mesh, PartitionSpec as P

bf16 = jnp.bfloat16
f32 = jnp.float32
i32 = jnp.int32
T = 128
ROWS = ("zh", "y")
COLS = ("zl", "x", "core")
BLOCKS = 32
SLOTS = 256
STRIDE = 320
PLACES = 1024
PART = 16
UNROLL = 32
NOWHERE = 31
LIMIT = 16 * 1024 * 1024


def spec(space=pltpu.VMEM):
    return pl.BlockSpec(memory_space=space)


def split_parts(value):
    high = value.astype(bf16)
    low = (value - high.astype(f32)).astype(bf16)
    return high, low


def ring_sum(own, received):
    return (own + received[1]) + (received[0] + received[2])


def local_kernel(inputs, message):
    n = (inputs.shape[0] - T) // 3
    og, pre, agg = (inputs[pl.ds(i * n, n), :] for i in range(3))
    weight = inputs[3 * n :, :]
    grad_pre = jnp.where(pre > 0, og, jnp.zeros_like(og))
    message[0:T, :] = lax.dot_general(
        weight, grad_pre, (((1,), (1,)), ((), ())), preferred_element_type=f32
    ).astype(bf16)
    partial = lax.dot_general(
        agg, grad_pre, (((0,), (0,)), ((), ())), preferred_element_type=f32
    )
    high, low = split_parts(partial)
    message[T : 2 * T, 0:T] = high
    message[T : 2 * T, T : 2 * T] = low


def chip_kernel(pos, own, other, message):
    core = pos[4]
    message[pl.ds(pl.multiple_of(core * T, T), T), :] = own[0:T, :]
    message[pl.ds(pl.multiple_of((1 - core) * T, T), T), :] = other[0:T, :]
    sums = [m[T : 2 * T, 0:T].astype(f32) + m[T : 2 * T, T : 2 * T].astype(f32) for m in (own, other)]
    total = (sums[0] + sums[1]).astype(bf16)
    message[2 * T : 2 * T + 64, 0:T] = total[0:64, :]
    message[2 * T : 2 * T + 64, T : 2 * T] = total[64:T, :]


def order_kernel(pos, count_ref, coords_hbm, tiles_hbm, out, tiles, coords, sems):
    fetches = [
        pltpu.make_async_copy(tiles_hbm.at[part], tiles.at[part], sems.at[1 + i])
        for i, part in enumerate(pl.ds(g * PART, PART) for g in range(SLOTS // PART))
    ]
    fetch_coords = pltpu.make_async_copy(coords_hbm, coords, sems.at[0])
    fetch_coords.start()
    count, y = count_ref[0], pos[1]
    for g, fetch in enumerate(fetches):
        pl.when(g * PART < count)(fetch.start)
    fetch_coords.wait()
    zh, turn = pos[0], 1 - 2 * pos[4]

    def place(k, ends):
        row, col = coords[0, k], coords[1, k]
        offset = ((((col >> 1) & 3) - y) * turn) & 3
        z_place = (((col >> 3) - zh) * turn + 2) & 3
        local = z_place * 2 + (col & 1) + jnp.where(offset == 3, 8, 0)
        stage = jnp.where(offset == 2, 0, jnp.where(offset == 0, 2, 1))
        end = jnp.where(offset == 2, ends[0], jnp.where(offset == 0, ends[2], ends[1]))
        out[0, end] = k + (row << 8) + (local << 16)
        return tuple(e + (stage == i).astype(i32) for i, e in enumerate(ends))

    starts = tuple(jnp.int32(STRIDE * i) for i in range(3))
    step = 8
    whole = count // step

    def several(i, ends):
        for u in range(step):
            ends = place(i * step + u, ends)
        return ends

    ends = lax.fori_loop(0, whole, several, starts)
    ends = lax.fori_loop(whole * step, count, place, ends)
    for i in range(3):
        for u in range(UNROLL):
            out[0, ends[i] + u] = NOWHERE << 16
        out[0, STRIDE * 3 + i] = (ends[i] - STRIDE * i + UNROLL - 1) // UNROLL
    for g, fetch in enumerate(fetches):
        pl.when(g * PART < count)(fetch.wait)


def multiply(stage, order, grads, tiles, acc):
    acc[...] = jnp.zeros_like(acc)
    spare = acc.shape[0] - 1

    @pl.loop(0, order[0, STRIDE * 3 + stage])
    def _(group):
        for u in range(UNROLL):
            code = order[0, STRIDE * stage + group * UNROLL + u]
            at = jnp.minimum(code >> 16, spare)
            acc[at] += jnp.dot(
                grads[(code >> 8) & 31], tiles[code & 255], preferred_element_type=f32
            )


def first_kernel(pos, order, *refs):
    mine, got, swapped = refs[0], refs[1:5], refs[5:9]
    tiles, grads, weight_part, send, acc, parts = refs[9:]
    zl, x, core = pos[2], pos[3], pos[4]

    arrived = [(got[k], core, k) for k in range(4)]
    arrived += [(swapped[k], 1 - core, k) for k in range(4)]
    arrived += [(mine, 0, 0)]
    for message, side, k in arrived:
        chip = ((zl + side) & 1) * 4 + ((x - k * (1 - 2 * side)) & 3)
        for c in range(2):
            for h in range(2):
                grads[chip * 4 + 2 * c + h] = message[c * T : (c + 1) * T, h * T : (h + 1) * T]
        parts[chip] = message[2 * T : 2 * T + 64, :]
    total = parts[0].astype(f32)
    for chip in range(1, 8):
        total += parts[chip].astype(f32)
    rounded = total.astype(bf16)
    weight_part[0:64, :] = rounded[:, 0:T]
    weight_part[64:T, :] = rounded[:, T : 2 * T]
    multiply(0, order, grads, tiles, acc)
    for i in range(8):
        send[i * T : (i + 1) * T, :] = acc[i].astype(bf16)
    send[8 * T : 9 * T, :] = weight_part[...]


def second_kernel(order, grads, weight_part, tiles, early_1, late_1, early_3, late_3, acc):
    multiply(1, order, grads, tiles, acc)
    for first, early, late in ((0, early_1, late_1), (8, early_3, late_3)):
        for i in range(4):
            early[i * T : (i + 1) * T, :] = acc[first + i].astype(bf16)
            late[i * T : (i + 1) * T, :] = acc[first + 4 + i].astype(bf16)
        early[4 * T : 5 * T, :] = weight_part[...]


def third_kernel(order, grads, tiles, after, early, late, acc):
    del after
    multiply(2, order, grads, tiles, acc)
    for i in range(4):
        early[i * T : (i + 1) * T, :] = acc[i]
        late[i * T : (i + 1) * T, :] = acc[4 + i]


def early_kernel(own, weight_part, r1, r2, r3, send_2, send_3, weight_y):
    parts = [r1[4 * T : 5 * T, :], r2[8 * T : 9 * T, :], r3[4 * T : 5 * T, :]]
    rounded = ring_sum(weight_part[...].astype(f32), [p.astype(f32) for p in parts]).astype(bf16)
    weight_y[...] = rounded
    for i, out in enumerate((send_2, send_3)):
        rows = pl.ds(i * 2 * T, 2 * T)
        total = own[rows, :]
        for r in (r1, r2, r3):
            total += r[rows, :].astype(f32)
        out[0 : 2 * T, :] = total.astype(bf16)
        out[2 * T : 3 * T, :] = rounded


def late_kernel(own, weight_y, r1, r2, r3, keep, send_1):
    for i, out in enumerate((keep, send_1)):
        rows = pl.ds(i * 2 * T, 2 * T)
        total = own[rows, :] + r2[(i + 2) * 2 * T : (i + 3) * 2 * T, :].astype(f32)
        for r in (r1, r3):
            total += r[rows, :].astype(f32)
        out[0 : 2 * T, :] = total.astype(out.dtype)
    send_1[2 * T : 3 * T, :] = weight_y[...]


def z_kernel(scale, keep, weight_y, r1, r2, r3, out, weight_out):
    parts = [r[2 * T : 3 * T, :].astype(f32) for r in (r1, r2, r3)]
    weight_out[...] = ring_sum(weight_y[...].astype(f32), parts) * scale
    for h in range(2):
        rows = pl.ds(h * T, T)
        total = keep[rows, :]
        for r in (r1, r2, r3):
            total += r[rows, :].astype(f32)
        out[rows, :] = total.T.astype(bf16)


def call(kernel, out_shape, in_specs, scratch=(), cost=None, out_specs=None):
    return pl.pallas_call(
        kernel,
        out_shape=out_shape,
        in_specs=in_specs,
        out_specs=out_specs or jax.tree.map(lambda _: spec(), out_shape),
        scratch_shapes=list(scratch),
        compiler_params=pltpu.CompilerParams(vmem_limit_bytes=LIMIT),
        cost_estimate=cost,
    )


def struct(*shape, dtype=bf16):
    return jax.ShapeDtypeStruct(shape, dtype)


def around(axis, value, d):
    pairs = [(i * 2, ((i + d) % 4) * 2) for i in range(4)]
    pairs += [(i * 2 + 1, ((i - d) % 4) * 2 + 1) for i in range(4)]
    return lax.ppermute(value, (axis, "core"), pairs)


def chip_perm(k):
    pairs = []
    for z in range(2):
        for x in range(4):
            at = (z * 4 + x) * 2
            if k:
                pairs.append((at, (z * 4 + (x + k) % 4) * 2))
            pairs.append((at + 1, ((1 - z) * 4 + (x - k) % 4) * 2 + 1))
    return pairs


def body(out_grad, preact, aggregated, weight, tiles, tile_coords, tile_count):
    smem, vmem, hbm = spec(pltpu.SMEM), spec(), spec(pltpu.HBM)
    nodes = out_grad.shape[0]
    pos = jnp.stack([lax.axis_index(a) for a in ROWS + COLS]).astype(i32)
    inputs = jnp.concatenate([out_grad, preact, aggregated, weight], 0)
    swap = [(0, 1), (1, 0)]
    local = call(local_kernel, struct(2 * T, nodes), [vmem])(inputs)
    mine = call(chip_kernel, struct(2 * T + 64, nodes), [smem, vmem, vmem])(
        pos, local, lax.ppermute(local, "core", swap)
    )
    order, held = call(
        order_kernel,
        [pltpu.SMEM((1, PLACES), i32), pltpu.VMEM((SLOTS, T, T), bf16)],
        [smem, smem, hbm, hbm],
        [pltpu.SMEM((2, SLOTS), i32), pltpu.SemaphoreType.DMA((1 + SLOTS // PART,))],
        pl.CostEstimate(flops=0, bytes_accessed=2 * SLOTS * T * T * 2, transcendentals=0),
        (smem, vmem),
    )(
        pos,
        tile_count.reshape(1),
        pltpu.with_memory_space_constraint(tile_coords.reshape(2, SLOTS), pltpu.HBM),
        pltpu.with_memory_space_constraint(tiles.reshape(SLOTS, T, T), pltpu.HBM),
    )
    got = [lax.ppermute(mine, COLS, chip_perm(k)) for k in range(4)]
    swapped = []
    for k in range(4):
        ready = got[k]
        if k == 3:
            ready, _ = lax.optimization_barrier((ready, order))
        swapped.append(lax.ppermute(ready, "core", swap))
    cost = lambda share: pl.CostEstimate(
        flops=share * SLOTS * 2 * T**3, bytes_accessed=share * SLOTS * T * T * 2, transcendentals=0
    )
    early, late, onward = struct(5 * T, T), struct(4 * T, T), struct(3 * T, T)
    grads, weight_part, send_2 = call(
        first_kernel,
        [struct(BLOCKS, T, T), struct(T, T), struct(9 * T, T)],
        [smem] * 2 + [vmem] * 10,
        [pltpu.VMEM((9, T, T), f32), pltpu.VMEM((8, 64, 2 * T), bf16)],
        cost(1),
    )(pos, order, mine, *got, *swapped, held)
    early_1, late_1, early_3, late_3 = call(
        second_kernel,
        [early, late] * 2,
        [smem] + [vmem] * 3,
        [pltpu.VMEM((17, T, T), f32)],
        cost(1),
    )(order, grads, weight_part, held)
    got_2 = around("y", send_2, 2)
    own_early, own_late = call(
        third_kernel,
        [struct(4 * T, T, dtype=f32)] * 2,
        [smem] + [vmem] * 2 + [spec(pl.ANY)],
        [pltpu.VMEM((9, T, T), f32)],
        cost(1),
    )(order, grads, held, early_1)
    got_early = [around("y", early_1, 1), got_2, around("y", early_3, 3)]
    got_late = [around("y", late_1, 1), got_2, around("y", late_3, 3)]
    send_2, send_3, weight_y = call(
        early_kernel, [onward, onward, struct(T, T)], [vmem] * 5, cost=cost(10)
    )(own_early, weight_part, *got_early)
    z_2, z_3 = around("zh", send_2, 2), around("zh", send_3, 3)
    keep, send_1 = call(late_kernel, [struct(2 * T, T, dtype=f32), onward], [vmem] * 5)(
        own_late, weight_y, *got_late
    )
    z_1 = around("zh", send_1, 1)
    devices = 1
    for a in ROWS + COLS:
        devices *= lax.axis_size(a)
    scale = 1.0 / (nodes * devices) ** 0.5
    input_grad, weight_grad = call(
        functools.partial(z_kernel, scale),
        [struct(nodes, T), struct(T, T, dtype=f32)],
        [vmem] * 5,
    )(keep, weight_y, z_1, z_2, z_3)
    return input_grad, weight_grad


def solution(mesh):
    fine = Mesh(mesh.devices.reshape(4, 4, 2, 4, 2), ROWS + COLS)
    every = ROWS + COLS
    return jax.shard_map(
        body,
        mesh=fine,
        in_specs=(
            P(every, None),
            P(every, None),
            P(every, None),
            P(),
            P(ROWS, COLS, None, None, None),
            P(ROWS, COLS, None, None),
            P(ROWS, COLS),
        ),
        out_specs=(P(every, None), P()),
        check_vma=False,
    )
```

```python
import functools

import jax
import jax.numpy as jnp
from jax import lax
from jax.experimental import pallas as pl
from jax.experimental.pallas import tpu as pltpu
from jax.sharding import Mesh, PartitionSpec as P

bf16 = jnp.bfloat16
f32 = jnp.float32
i32 = jnp.int32
T = 128
ROWS = ("zh", "y")
COLS = ("zl", "x", "core")
BLOCKS = 32
SLOTS = 256
STRIDE = 320
PLACES = 1024
PART = 16
UNROLL = 32
NOWHERE = 31
LIMIT = 16 * 1024 * 1024


def spec(space=pltpu.VMEM):
    return pl.BlockSpec(memory_space=space)


def split_parts(value):
    high = value.astype(bf16)
    low = (value - high.astype(f32)).astype(bf16)
    return high, low


def ring_sum(own, received):
    return (own + received[1]) + (received[0] + received[2])


def local_kernel(inputs, message):
    n = (inputs.shape[0] - T) // 3
    og, pre, agg = (inputs[pl.ds(i * n, n), :] for i in range(3))
    weight = inputs[3 * n :, :]
    grad_pre = jnp.where(pre > 0, og, jnp.zeros_like(og))
    message[0:T, :] = lax.dot_general(
        weight, grad_pre, (((1,), (1,)), ((), ())), preferred_element_type=f32
    ).astype(bf16)
    partial = lax.dot_general(
        agg, grad_pre, (((0,), (0,)), ((), ())), preferred_element_type=f32
    )
    high, low = split_parts(partial)
    message[T : 2 * T, 0:T] = high
    message[T : 2 * T, T : 2 * T] = low


def chip_kernel(pos, own, other, message):
    core = pos[4]
    message[pl.ds(pl.multiple_of(core * T, T), T), :] = own[0:T, :]
    message[pl.ds(pl.multiple_of((1 - core) * T, T), T), :] = other[0:T, :]
    sums = [m[T : 2 * T, 0:T].astype(f32) + m[T : 2 * T, T : 2 * T].astype(f32) for m in (own, other)]
    total = (sums[0] + sums[1]).astype(bf16)
    message[2 * T : 2 * T + 64, 0:T] = total[0:64, :]
    message[2 * T : 2 * T + 64, T : 2 * T] = total[64:T, :]


def order_kernel(pos, count_ref, coords_hbm, tiles_hbm, out, tiles, coords, sems):
    fetches = [
        pltpu.make_async_copy(tiles_hbm.at[part], tiles.at[part], sems.at[1 + i])
        for i, part in enumerate(pl.ds(g * PART, PART) for g in range(SLOTS // PART))
    ]
    fetch_coords = pltpu.make_async_copy(coords_hbm, coords, sems.at[0])
    fetch_coords.start()
    count, y = count_ref[0], pos[1]
    for g, fetch in enumerate(fetches):
        pl.when(g * PART < count)(fetch.start)
    fetch_coords.wait()
    zh, turn = pos[0], 1 - 2 * pos[4]

    def place(k, ends):
        row, col = coords[0, k], coords[1, k]
        offset = ((((col >> 1) & 3) - y) * turn) & 3
        z_place = (((col >> 3) - zh) * turn + 2) & 3
        local = z_place * 2 + (col & 1) + jnp.where(offset == 3, 8, 0)
        stage = jnp.where(offset == 2, 0, jnp.where(offset == 0, 2, 1))
        end = jnp.where(offset == 2, ends[0], jnp.where(offset == 0, ends[2], ends[1]))
        out[0, end] = k + (row << 8) + (local << 16)
        return tuple(e + (stage == i).astype(i32) for i, e in enumerate(ends))

    starts = tuple(jnp.int32(STRIDE * i) for i in range(3))
    step = 8
    whole = count // step

    def several(i, ends):
        for u in range(step):
            ends = place(i * step + u, ends)
        return ends

    ends = lax.fori_loop(0, whole, several, starts)
    ends = lax.fori_loop(whole * step, count, place, ends)
    for i in range(3):
        for u in range(UNROLL):
            out[0, ends[i] + u] = NOWHERE << 16
        out[0, STRIDE * 3 + i] = (ends[i] - STRIDE * i + UNROLL - 1) // UNROLL
    for g, fetch in enumerate(fetches):
        pl.when(g * PART < count)(fetch.wait)


def multiply(stage, order, grads, tiles, acc):
    acc[...] = jnp.zeros_like(acc)
    spare = acc.shape[0] - 1

    @pl.loop(0, order[0, STRIDE * 3 + stage])
    def _(group):
        for u in range(UNROLL):
            code = order[0, STRIDE * stage + group * UNROLL + u]
            at = jnp.minimum(code >> 16, spare)
            acc[at] += jnp.dot(
                grads[(code >> 8) & 31], tiles[code & 255], preferred_element_type=f32
            )


def put(acc, first, early, late):
    for i in range(4):
        early[i * T : (i + 1) * T, :] = acc[first + i].astype(early.dtype)
        late[i * T : (i + 1) * T, :] = acc[first + 4 + i].astype(late.dtype)


def first_kernel(pos, order, *refs):
    mine, got, swapped = refs[0], refs[1:5], refs[5:9]
    tiles, grads, weight_part, early, late, acc, parts = refs[9:]
    zl, x, core = pos[2], pos[3], pos[4]

    arrived = [(got[k], core, k) for k in range(4)]
    arrived += [(swapped[k], 1 - core, k) for k in range(4)]
    arrived += [(mine, 0, 0)]
    for message, side, k in arrived:
        chip = ((zl + side) & 1) * 4 + ((x - k * (1 - 2 * side)) & 3)
        for c in range(2):
            for h in range(2):
                grads[chip * 4 + 2 * c + h] = message[c * T : (c + 1) * T, h * T : (h + 1) * T]
        parts[chip] = message[2 * T : 2 * T + 64, :]
    total = parts[0].astype(f32)
    for chip in range(1, 8):
        total += parts[chip].astype(f32)
    rounded = total.astype(bf16)
    weight_part[0:64, :] = rounded[:, 0:T]
    weight_part[64:T, :] = rounded[:, T : 2 * T]
    multiply(0, order, grads, tiles, acc)
    put(acc, 0, early, late)
    early[4 * T : 5 * T, :] = weight_part[...]


def second_kernel(order, grads, weight_part, tiles, early_1, late_1, early_3, late_3, acc):
    multiply(1, order, grads, tiles, acc)
    for first, early, late in ((0, early_1, late_1), (8, early_3, late_3)):
        put(acc, first, early, late)
        early[4 * T : 5 * T, :] = weight_part[...]


def third_kernel(order, grads, tiles, after, early, late, acc):
    del after
    multiply(2, order, grads, tiles, acc)
    put(acc, 0, early, late)


def early_kernel(own, weight_part, r1, r2, r3, send_2, send_3, weight_y):
    parts = [r[4 * T : 5 * T, :].astype(f32) for r in (r1, r2, r3)]
    rounded = ring_sum(weight_part[...].astype(f32), parts).astype(bf16)
    weight_y[...] = rounded
    for i, out in enumerate((send_2, send_3)):
        rows = pl.ds(i * 2 * T, 2 * T)
        total = own[rows, :]
        for r in (r1, r2, r3):
            total += r[rows, :].astype(f32)
        out[0 : 2 * T, :] = total.astype(bf16)
        out[2 * T : 3 * T, :] = rounded


def late_kernel(own, weight_y, r1, r2, r3, keep, send_1):
    for i, out in enumerate((keep, send_1)):
        rows = pl.ds(i * 2 * T, 2 * T)
        total = own[rows, :]
        for r in (r1, r2, r3):
            total += r[rows, :].astype(f32)
        out[0 : 2 * T, :] = total.astype(out.dtype)
    send_1[2 * T : 3 * T, :] = weight_y[...]


def z_kernel(scale, keep, weight_y, r1, r2, r3, out, weight_out):
    parts = [r[2 * T : 3 * T, :].astype(f32) for r in (r1, r2, r3)]
    weight_out[...] = ring_sum(weight_y[...].astype(f32), parts) * scale
    for h in range(2):
        rows = pl.ds(h * T, T)
        total = keep[rows, :]
        for r in (r1, r2, r3):
            total += r[rows, :].astype(f32)
        out[rows, :] = total.T.astype(bf16)


def call(kernel, out_shape, in_specs, scratch=(), cost=None, out_specs=None):
    return pl.pallas_call(
        kernel,
        out_shape=out_shape,
        in_specs=in_specs,
        out_specs=out_specs or jax.tree.map(lambda _: spec(), out_shape),
        scratch_shapes=list(scratch),
        compiler_params=pltpu.CompilerParams(vmem_limit_bytes=LIMIT),
        cost_estimate=cost,
    )


def struct(*shape, dtype=bf16):
    return jax.ShapeDtypeStruct(shape, dtype)


def around(axis, value, d):
    pairs = [(i * 2, ((i + d) % 4) * 2) for i in range(4)]
    pairs += [(i * 2 + 1, ((i - d) % 4) * 2 + 1) for i in range(4)]
    return lax.ppermute(value, (axis, "core"), pairs)


def chip_perm(k):
    pairs = []
    for z in range(2):
        for x in range(4):
            at = (z * 4 + x) * 2
            if k:
                pairs.append((at, (z * 4 + (x + k) % 4) * 2))
            pairs.append((at + 1, ((1 - z) * 4 + (x - k) % 4) * 2 + 1))
    return pairs


def body(out_grad, preact, aggregated, weight, tiles, tile_coords, tile_count):
    smem, vmem, hbm = spec(pltpu.SMEM), spec(), spec(pltpu.HBM)
    nodes = out_grad.shape[0]
    pos = jnp.stack([lax.axis_index(a) for a in ROWS + COLS]).astype(i32)
    inputs = jnp.concatenate([out_grad, preact, aggregated, weight], 0)
    swap = [(0, 1), (1, 0)]
    local = call(local_kernel, struct(2 * T, nodes), [vmem])(inputs)
    mine = call(chip_kernel, struct(2 * T + 64, nodes), [smem, vmem, vmem])(
        pos, local, lax.ppermute(local, "core", swap)
    )
    order, held = call(
        order_kernel,
        [pltpu.SMEM((1, PLACES), i32), pltpu.VMEM((SLOTS, T, T), bf16)],
        [smem, smem, hbm, hbm],
        [pltpu.SMEM((2, SLOTS), i32), pltpu.SemaphoreType.DMA((1 + SLOTS // PART,))],
        pl.CostEstimate(flops=0, bytes_accessed=2 * SLOTS * T * T * 2, transcendentals=0),
        (smem, vmem),
    )(
        pos,
        tile_count.reshape(1),
        pltpu.with_memory_space_constraint(tile_coords.reshape(2, SLOTS), pltpu.HBM),
        pltpu.with_memory_space_constraint(tiles.reshape(SLOTS, T, T), pltpu.HBM),
    )
    got = [lax.ppermute(mine, COLS, chip_perm(k)) for k in range(4)]
    swapped = []
    for k in range(4):
        ready = got[k]
        if k == 3:
            ready, _ = lax.optimization_barrier((ready, order))
        swapped.append(lax.ppermute(ready, "core", swap))
    cost = lambda share: pl.CostEstimate(
        flops=share * SLOTS * 2 * T**3, bytes_accessed=share * SLOTS * T * T * 2, transcendentals=0
    )
    early, late, onward = struct(5 * T, T), struct(4 * T, T), struct(3 * T, T)
    grads, weight_part, early_2, late_2 = call(
        first_kernel,
        [struct(BLOCKS, T, T), struct(T, T), early, late],
        [smem] * 2 + [vmem] * 10,
        [pltpu.VMEM((9, T, T), f32), pltpu.VMEM((8, 64, 2 * T), bf16)],
        cost(1),
    )(pos, order, mine, *got, *swapped, held)
    early_1, late_1, early_3, late_3 = call(
        second_kernel,
        [early, late] * 2,
        [smem] + [vmem] * 3,
        [pltpu.VMEM((17, T, T), f32)],
        cost(1),
    )(order, grads, weight_part, held)
    own_early, own_late = call(
        third_kernel,
        [struct(4 * T, T, dtype=f32)] * 2,
        [smem] + [vmem] * 2 + [spec(pl.ANY)],
        [pltpu.VMEM((9, T, T), f32)],
        cost(1),
    )(order, grads, held, early_1)
    got_early = [around("y", v, d) for d, v in ((1, early_1), (2, early_2), (3, early_3))]
    got_late = [around("y", v, d) for d, v in ((1, late_1), (2, late_2), (3, late_3))]
    send_2, send_3, weight_y = call(
        early_kernel, [onward, onward, struct(T, T)], [vmem] * 5, cost=cost(10)
    )(own_early, weight_part, *got_early)
    z_2, z_3 = around("zh", send_2, 2), around("zh", send_3, 3)
    keep, send_1 = call(late_kernel, [struct(2 * T, T, dtype=f32), onward], [vmem] * 5)(
        own_late, weight_y, *got_late
    )
    z_1 = around("zh", send_1, 1)
    devices = 1
    for a in ROWS + COLS:
        devices *= lax.axis_size(a)
    scale = 1.0 / (nodes * devices) ** 0.5
    input_grad, weight_grad = call(
        functools.partial(z_kernel, scale),
        [struct(nodes, T), struct(T, T, dtype=f32)],
        [vmem] * 5,
    )(keep, weight_y, z_1, z_2, z_3)
    return input_grad, weight_grad


def solution(mesh):
    fine = Mesh(mesh.devices.reshape(4, 4, 2, 4, 2), ROWS + COLS)
    every = ROWS + COLS
    return jax.shard_map(
        body,
        mesh=fine,
        in_specs=(
            P(every, None),
            P(every, None),
            P(every, None),
            P(),
            P(ROWS, COLS, None, None, None),
            P(ROWS, COLS, None, None),
            P(ROWS, COLS),
        ),
        out_specs=(P(every, None), P()),
        check_vma=False,
    )
```

```python
import functools

import jax
import jax.numpy as jnp
from jax import lax
from jax.experimental import pallas as pl
from jax.experimental.pallas import tpu as pltpu
from jax.sharding import Mesh, PartitionSpec as P

bf16 = jnp.bfloat16
f32 = jnp.float32
i32 = jnp.int32
T = 128
ROWS = ("zh", "y")
COLS = ("zl", "x", "core")
BLOCKS = 32
SLOTS = 256
STRIDE = 320
PLACES = 1024
PART = 16
UNROLL = 32
NOWHERE = 31
LIMIT = 16 * 1024 * 1024


def spec(space=pltpu.VMEM):
    return pl.BlockSpec(memory_space=space)


def split_parts(value):
    high = value.astype(bf16)
    low = (value - high.astype(f32)).astype(bf16)
    return high, low


def ring_sum(own, received):
    return (own + received[1]) + (received[0] + received[2])


def local_kernel(inputs, message):
    n = (inputs.shape[0] - T) // 3
    og, pre, agg = (inputs[pl.ds(i * n, n), :] for i in range(3))
    weight = inputs[3 * n :, :]
    grad_pre = jnp.where(pre > 0, og, jnp.zeros_like(og))
    message[0:T, :] = lax.dot_general(
        weight, grad_pre, (((1,), (1,)), ((), ())), preferred_element_type=f32
    ).astype(bf16)
    partial = lax.dot_general(
        agg, grad_pre, (((0,), (0,)), ((), ())), preferred_element_type=f32
    )
    high, low = split_parts(partial)
    message[T : 2 * T, 0:T] = high
    message[T : 2 * T, T : 2 * T] = low


def chip_kernel(pos, own, other, message):
    core = pos[4]
    message[pl.ds(pl.multiple_of(core * T, T), T), :] = own[0:T, :]
    message[pl.ds(pl.multiple_of((1 - core) * T, T), T), :] = other[0:T, :]
    sums = [m[T : 2 * T, 0:T].astype(f32) + m[T : 2 * T, T : 2 * T].astype(f32) for m in (own, other)]
    total = (sums[0] + sums[1]).astype(bf16)
    message[2 * T : 2 * T + 64, 0:T] = total[0:64, :]
    message[2 * T : 2 * T + 64, T : 2 * T] = total[64:T, :]


def order_kernel(pos, count_ref, coords_hbm, tiles_hbm, out, tiles, coords, sems):
    fetches = [
        pltpu.make_async_copy(tiles_hbm.at[part], tiles.at[part], sems.at[1 + i])
        for i, part in enumerate(pl.ds(g * PART, PART) for g in range(SLOTS // PART))
    ]
    fetch_coords = pltpu.make_async_copy(coords_hbm, coords, sems.at[0])
    fetch_coords.start()
    count, y = count_ref[0], pos[1]
    for g, fetch in enumerate(fetches):
        pl.when(g * PART < count)(fetch.start)
    fetch_coords.wait()
    zh, turn = pos[0], 1 - 2 * pos[4]

    def place(k, ends):
        row, col = coords[0, k], coords[1, k]
        offset = ((((col >> 1) & 3) - y) * turn) & 3
        z_place = (((col >> 3) - zh) * turn + 2) & 3
        local = z_place * 2 + (col & 1) + jnp.where(offset == 3, 8, 0)
        stage = jnp.where(offset == 2, 0, jnp.where(offset == 0, 2, 1))
        end = jnp.where(offset == 2, ends[0], jnp.where(offset == 0, ends[2], ends[1]))
        out[0, end] = k + (row << 8) + (local << 16)
        return tuple(e + (stage == i).astype(i32) for i, e in enumerate(ends))

    starts = tuple(jnp.int32(STRIDE * i) for i in range(3))
    step = 8
    whole = count // step

    def several(i, ends):
        for u in range(step):
            ends = place(i * step + u, ends)
        return ends

    ends = lax.fori_loop(0, whole, several, starts)
    ends = lax.fori_loop(whole * step, count, place, ends)
    for i in range(3):
        for u in range(UNROLL):
            out[0, ends[i] + u] = NOWHERE << 16
        out[0, STRIDE * 3 + i] = (ends[i] - STRIDE * i + UNROLL - 1) // UNROLL
    for g, fetch in enumerate(fetches):
        pl.when(g * PART < count)(fetch.wait)


def multiply(stage, order, grads, tiles, acc):
    acc[...] = jnp.zeros_like(acc)
    spare = acc.shape[0] - 1

    @pl.loop(0, order[0, STRIDE * 3 + stage])
    def _(group):
        for u in range(UNROLL):
            code = order[0, STRIDE * stage + group * UNROLL + u]
            at = jnp.minimum(code >> 16, spare)
            acc[at] += jnp.dot(
                grads[(code >> 8) & 31], tiles[code & 255], preferred_element_type=f32
            )


def put(acc, first, early, late):
    for i in range(4):
        early[i * T : (i + 1) * T, :] = acc[first + i].astype(early.dtype)
        late[i * T : (i + 1) * T, :] = acc[first + 4 + i].astype(late.dtype)


def first_kernel(pos, order, *refs):
    mine, got, swapped = refs[0], refs[1:5], refs[5:9]
    tiles, grads, weight_part, early, late, acc, parts = refs[9:]
    zl, x, core = pos[2], pos[3], pos[4]

    arrived = [(got[k], core, k) for k in range(4)]
    arrived += [(swapped[k], 1 - core, k) for k in range(4)]
    arrived += [(mine, 0, 0)]
    for message, side, k in arrived:
        chip = ((zl + side) & 1) * 4 + ((x - k * (1 - 2 * side)) & 3)
        for c in range(2):
            for h in range(2):
                grads[chip * 4 + 2 * c + h] = message[c * T : (c + 1) * T, h * T : (h + 1) * T]
        parts[chip] = message[2 * T : 2 * T + 64, :]
    total = parts[0].astype(f32)
    for chip in range(1, 8):
        total += parts[chip].astype(f32)
    rounded = total.astype(bf16)
    weight_part[0:64, :] = rounded[:, 0:T]
    weight_part[64:T, :] = rounded[:, T : 2 * T]
    multiply(0, order, grads, tiles, acc)
    put(acc, 0, early, late)
    early[4 * T : 5 * T, :] = weight_part[...]


def second_kernel(order, grads, weight_part, tiles, early_1, late_1, early_3, late_3, acc):
    multiply(1, order, grads, tiles, acc)
    for first, early, late in ((0, early_1, late_1), (8, early_3, late_3)):
        put(acc, first, early, late)
        early[4 * T : 5 * T, :] = weight_part[...]


def third_kernel(order, grads, tiles, after, early, late, acc):
    del after
    multiply(2, order, grads, tiles, acc)
    put(acc, 0, early, late)


def early_kernel(own, weight_part, r1, r2, r3, send_2, send_3, weight_y):
    parts = [r[4 * T : 5 * T, :].astype(f32) for r in (r1, r2, r3)]
    rounded = ring_sum(weight_part[...].astype(f32), parts).astype(bf16)
    weight_y[...] = rounded
    for i, out in enumerate((send_2, send_3)):
        rows = pl.ds(i * 2 * T, 2 * T)
        total = own[rows, :]
        for r in (r1, r2, r3):
            total += r[rows, :].astype(f32)
        out[0 : 2 * T, :] = total.astype(bf16)
        out[2 * T : 3 * T, :] = rounded


def late_kernel(own, weight_y, r1, r2, r3, keep, send_1):
    for i, out in enumerate((keep, send_1)):
        rows = pl.ds(i * 2 * T, 2 * T)
        total = own[rows, :]
        for r in (r1, r2, r3):
            total += r[rows, :].astype(f32)
        out[0 : 2 * T, :] = total.astype(out.dtype)
    send_1[2 * T : 3 * T, :] = weight_y[...]


def z_kernel(scale, keep, weight_y, r1, r2, r3, out, weight_out):
    parts = [r[2 * T : 3 * T, :].astype(f32) for r in (r1, r2, r3)]
    weight_out[...] = ring_sum(weight_y[...].astype(f32), parts) * scale
    for h in range(2):
        rows = pl.ds(h * T, T)
        total = keep[rows, :]
        for r in (r1, r2, r3):
            total += r[rows, :].astype(f32)
        out[rows, :] = total.T.astype(bf16)


def call(kernel, out_shape, in_specs, scratch=(), cost=None, out_specs=None):
    return pl.pallas_call(
        kernel,
        out_shape=out_shape,
        in_specs=in_specs,
        out_specs=out_specs or jax.tree.map(lambda _: spec(), out_shape),
        scratch_shapes=list(scratch),
        compiler_params=pltpu.CompilerParams(vmem_limit_bytes=LIMIT),
        cost_estimate=cost,
    )


def struct(*shape, dtype=bf16):
    return jax.ShapeDtypeStruct(shape, dtype)


def around(axis, value, d):
    pairs = [(i * 2, ((i + d) % 4) * 2) for i in range(4)]
    pairs += [(i * 2 + 1, ((i - d) % 4) * 2 + 1) for i in range(4)]
    return lax.ppermute(value, (axis, "core"), pairs)


def chip_perm(k):
    pairs = []
    for z in range(2):
        for x in range(4):
            at = (z * 4 + x) * 2
            if k:
                pairs.append((at, (z * 4 + (x + k) % 4) * 2))
            pairs.append((at + 1, ((1 - z) * 4 + (x - k) % 4) * 2 + 1))
    return pairs


def body(out_grad, preact, aggregated, weight, tiles, tile_coords, tile_count):
    smem, vmem, hbm = spec(pltpu.SMEM), spec(), spec(pltpu.HBM)
    nodes = out_grad.shape[0]
    pos = jnp.stack([lax.axis_index(a) for a in ROWS + COLS]).astype(i32)
    inputs = jnp.concatenate([out_grad, preact, aggregated, weight], 0)
    swap = [(0, 1), (1, 0)]
    local = call(local_kernel, struct(2 * T, nodes), [vmem])(inputs)
    mine = call(chip_kernel, struct(2 * T + 64, nodes), [smem, vmem, vmem])(
        pos, local, lax.ppermute(local, "core", swap)
    )
    order, held = call(
        order_kernel,
        [pltpu.SMEM((1, PLACES), i32), pltpu.VMEM((SLOTS, T, T), bf16)],
        [smem, smem, hbm, hbm],
        [pltpu.SMEM((2, SLOTS), i32), pltpu.SemaphoreType.DMA((1 + SLOTS // PART,))],
        pl.CostEstimate(flops=0, bytes_accessed=2 * SLOTS * T * T * 2, transcendentals=0),
        (smem, vmem),
    )(
        pos,
        tile_count.reshape(1),
        pltpu.with_memory_space_constraint(tile_coords.reshape(2, SLOTS), pltpu.HBM),
        pltpu.with_memory_space_constraint(tiles.reshape(SLOTS, T, T), pltpu.HBM),
    )
    got = [lax.ppermute(mine, COLS, chip_perm(k)) for k in range(4)]
    swapped = []
    for k in range(4):
        ready = got[k]
        if k == 2:
            ready, _ = lax.optimization_barrier((ready, order))
        swapped.append(lax.ppermute(ready, "core", swap))
    cost = lambda share: pl.CostEstimate(
        flops=share * SLOTS * 2 * T**3, bytes_accessed=share * SLOTS * T * T * 2, transcendentals=0
    )
    early, late, onward = struct(5 * T, T), struct(4 * T, T), struct(3 * T, T)
    grads, weight_part, early_2, late_2 = call(
        first_kernel,
        [struct(BLOCKS, T, T), struct(T, T), early, late],
        [smem] * 2 + [vmem] * 10,
        [pltpu.VMEM((9, T, T), f32), pltpu.VMEM((8, 64, 2 * T), bf16)],
        cost(1),
    )(pos, order, mine, *got, *swapped, held)
    early_1, late_1, early_3, late_3 = call(
        second_kernel,
        [early, late] * 2,
        [smem] + [vmem] * 3,
        [pltpu.VMEM((17, T, T), f32)],
        cost(1),
    )(order, grads, weight_part, held)
    own_early, own_late = call(
        third_kernel,
        [struct(4 * T, T, dtype=f32)] * 2,
        [smem] + [vmem] * 2 + [spec(pl.ANY)],
        [pltpu.VMEM((9, T, T), f32)],
        cost(1),
    )(order, grads, held, early_1)
    got_early = [around("y", v, d) for d, v in ((1, early_1), (2, early_2), (3, early_3))]
    got_late = [around("y", v, d) for d, v in ((1, late_1), (2, late_2), (3, late_3))]
    send_2, send_3, weight_y = call(
        early_kernel, [onward, onward, struct(T, T)], [vmem] * 5, cost=cost(10)
    )(own_early, weight_part, *got_early)
    z_2, z_3 = around("zh", send_2, 2), around("zh", send_3, 3)
    keep, send_1 = call(late_kernel, [struct(2 * T, T, dtype=f32), onward], [vmem] * 5)(
        own_late, weight_y, *got_late
    )
    z_1 = around("zh", send_1, 1)
    devices = 1
    for a in ROWS + COLS:
        devices *= lax.axis_size(a)
    scale = 1.0 / (nodes * devices) ** 0.5
    input_grad, weight_grad = call(
        functools.partial(z_kernel, scale),
        [struct(nodes, T), struct(T, T, dtype=f32)],
        [vmem] * 5,
    )(keep, weight_y, z_1, z_2, z_3)
    return input_grad, weight_grad


def solution(mesh):
    fine = Mesh(mesh.devices.reshape(4, 4, 2, 4, 2), ROWS + COLS)
    every = ROWS + COLS
    return jax.shard_map(
        body,
        mesh=fine,
        in_specs=(
            P(every, None),
            P(every, None),
            P(every, None),
            P(),
            P(ROWS, COLS, None, None, None),
            P(ROWS, COLS, None, None),
            P(ROWS, COLS),
        ),
        out_specs=(P(every, None), P()),
        check_vma=False,
    )
```

```python
import functools

import jax
import jax.numpy as jnp
from jax import lax
from jax.experimental import pallas as pl
from jax.experimental.pallas import tpu as pltpu
from jax.sharding import Mesh, PartitionSpec as P

bf16 = jnp.bfloat16
f32 = jnp.float32
i32 = jnp.int32
T = 128
ROWS = ("zh", "y")
COLS = ("zl", "x", "core")
BLOCKS = 32
SLOTS = 256
STRIDE = 320
PLACES = 1024
PART = 16
UNROLL = 32
NOWHERE = 31
LIMIT = 16 * 1024 * 1024


def spec(space=pltpu.VMEM):
    return pl.BlockSpec(memory_space=space)


def split_parts(value):
    high = value.astype(bf16)
    low = (value - high.astype(f32)).astype(bf16)
    return high, low


def ring_sum(own, received):
    return (own + received[1]) + (received[0] + received[2])


def local_kernel(inputs, message):
    n = (inputs.shape[0] - T) // 3
    og, pre, agg = (inputs[pl.ds(i * n, n), :] for i in range(3))
    weight = inputs[3 * n :, :]
    grad_pre = jnp.where(pre > 0, og, jnp.zeros_like(og))
    message[0:T, :] = lax.dot_general(
        weight, grad_pre, (((1,), (1,)), ((), ())), preferred_element_type=f32
    ).astype(bf16)
    partial = lax.dot_general(
        agg, grad_pre, (((0,), (0,)), ((), ())), preferred_element_type=f32
    )
    high, low = split_parts(partial)
    message[T : 2 * T, 0:T] = high
    message[T : 2 * T, T : 2 * T] = low


def chip_kernel(pos, own, other, message):
    core = pos[4]
    message[pl.ds(pl.multiple_of(core * T, T), T), :] = own[0:T, :]
    message[pl.ds(pl.multiple_of((1 - core) * T, T), T), :] = other[0:T, :]
    sums = [m[T : 2 * T, 0:T].astype(f32) + m[T : 2 * T, T : 2 * T].astype(f32) for m in (own, other)]
    total = (sums[0] + sums[1]).astype(bf16)
    message[2 * T : 2 * T + 64, 0:T] = total[0:64, :]
    message[2 * T : 2 * T + 64, T : 2 * T] = total[64:T, :]


def order_kernel(pos, count_ref, coords_hbm, tiles_hbm, out, tiles, coords, sems):
    fetches = [
        pltpu.make_async_copy(tiles_hbm.at[part], tiles.at[part], sems.at[1 + i])
        for i, part in enumerate(pl.ds(g * PART, PART) for g in range(SLOTS // PART))
    ]
    fetch_coords = pltpu.make_async_copy(coords_hbm, coords, sems.at[0])
    fetch_coords.start()
    count, y = count_ref[0], pos[1]
    for g, fetch in enumerate(fetches):
        pl.when(g * PART < count)(fetch.start)
    fetch_coords.wait()
    zh, turn = pos[0], 1 - 2 * pos[4]

    def place(k, ends):
        row, col = coords[0, k], coords[1, k]
        offset = ((((col >> 1) & 3) - y) * turn) & 3
        z_place = (((col >> 3) - zh) * turn + 2) & 3
        local = z_place * 2 + (col & 1) + jnp.where(offset == 3, 8, 0)
        stage = jnp.where(offset == 2, 0, jnp.where(offset == 0, 2, 1))
        end = jnp.where(offset == 2, ends[0], jnp.where(offset == 0, ends[2], ends[1]))
        out[0, end] = k + (row << 8) + (local << 16)
        return tuple(e + (stage == i).astype(i32) for i, e in enumerate(ends))

    starts = tuple(jnp.int32(STRIDE * i) for i in range(3))
    step = 8
    whole = count // step

    def several(i, ends):
        for u in range(step):
            ends = place(i * step + u, ends)
        return ends

    ends = lax.fori_loop(0, whole, several, starts)
    ends = lax.fori_loop(whole * step, count, place, ends)
    for i in range(3):
        for u in range(UNROLL):
            out[0, ends[i] + u] = NOWHERE << 16
        out[0, STRIDE * 3 + i] = (ends[i] - STRIDE * i + UNROLL - 1) // UNROLL
    for g, fetch in enumerate(fetches):
        pl.when(g * PART < count)(fetch.wait)


def multiply(stage, order, grads, tiles, acc):
    acc[...] = jnp.zeros_like(acc)
    spare = acc.shape[0] - 1

    @pl.loop(0, order[0, STRIDE * 3 + stage])
    def _(group):
        for u in range(UNROLL):
            code = order[0, STRIDE * stage + group * UNROLL + u]
            at = jnp.minimum(code >> 16, spare)
            acc[at] += jnp.dot(
                grads[(code >> 8) & 31], tiles[code & 255], preferred_element_type=f32
            )


def put(acc, first, early, late):
    for i in range(4):
        early[i * T : (i + 1) * T, :] = acc[first + i].astype(early.dtype)
        late[i * T : (i + 1) * T, :] = acc[first + 4 + i].astype(late.dtype)


def first_kernel(pos, order, *refs):
    mine, got, swapped = refs[0], refs[1:5], refs[5:9]
    tiles, grads, weight_part, early, late, acc, parts = refs[9:]
    zl, x, core = pos[2], pos[3], pos[4]

    arrived = [(got[k], core, k) for k in range(4)]
    arrived += [(swapped[k], 1 - core, k) for k in range(4)]
    arrived += [(mine, 0, 0)]
    for message, side, k in arrived:
        chip = ((zl + side) & 1) * 4 + ((x - k * (1 - 2 * side)) & 3)
        for c in range(2):
            for h in range(2):
                grads[chip * 4 + 2 * c + h] = message[c * T : (c + 1) * T, h * T : (h + 1) * T]
        parts[chip] = message[2 * T : 2 * T + 64, :]
    total = parts[0].astype(f32)
    for chip in range(1, 8):
        total += parts[chip].astype(f32)
    rounded = total.astype(bf16)
    weight_part[0:64, :] = rounded[:, 0:T]
    weight_part[64:T, :] = rounded[:, T : 2 * T]
    multiply(0, order, grads, tiles, acc)
    put(acc, 0, early, late)
    early[4 * T : 5 * T, :] = weight_part[...]


def second_kernel(order, grads, weight_part, tiles, early_1, late_1, early_3, late_3, acc):
    multiply(1, order, grads, tiles, acc)
    for first, early, late in ((0, early_1, late_1), (8, early_3, late_3)):
        put(acc, first, early, late)
        early[4 * T : 5 * T, :] = weight_part[...]


def third_kernel(order, grads, tiles, after, early, late, acc):
    del after
    multiply(2, order, grads, tiles, acc)
    put(acc, 0, early, late)


def early_kernel(own, weight_part, r1, r2, r3, send_2, send_3, weight_y):
    parts = [r[4 * T : 5 * T, :].astype(f32) for r in (r1, r2, r3)]
    rounded = ring_sum(weight_part[...].astype(f32), parts).astype(bf16)
    weight_y[...] = rounded
    for i, out in enumerate((send_2, send_3)):
        rows = pl.ds(i * 2 * T, 2 * T)
        total = own[rows, :]
        for r in (r1, r2, r3):
            total += r[rows, :].astype(f32)
        out[0 : 2 * T, :] = total.astype(bf16)
        out[2 * T : 3 * T, :] = rounded


def late_kernel(own, weight_y, r1, r2, r3, keep, send_1):
    for i, out in enumerate((keep, send_1)):
        rows = pl.ds(i * 2 * T, 2 * T)
        total = own[rows, :]
        for r in (r1, r2, r3):
            total += r[rows, :].astype(f32)
        out[0 : 2 * T, :] = total.astype(out.dtype)
    send_1[2 * T : 3 * T, :] = weight_y[...]


def z_kernel(scale, keep, weight_y, r1, r2, r3, out, weight_out):
    parts = [r[2 * T : 3 * T, :].astype(f32) for r in (r1, r2, r3)]
    weight_out[...] = ring_sum(weight_y[...].astype(f32), parts) * scale
    for h in range(2):
        rows = pl.ds(h * T, T)
        total = keep[rows, :]
        for r in (r1, r2, r3):
            total += r[rows, :].astype(f32)
        out[rows, :] = total.T.astype(bf16)


def call(kernel, out_shape, in_specs, scratch=(), cost=None, out_specs=None):
    return pl.pallas_call(
        kernel,
        out_shape=out_shape,
        in_specs=in_specs,
        out_specs=out_specs or jax.tree.map(lambda _: spec(), out_shape),
        scratch_shapes=list(scratch),
        compiler_params=pltpu.CompilerParams(vmem_limit_bytes=LIMIT),
        cost_estimate=cost,
    )


def struct(*shape, dtype=bf16):
    return jax.ShapeDtypeStruct(shape, dtype)


def around(axis, value, d):
    pairs = [(i * 2, ((i + d) % 4) * 2) for i in range(4)]
    pairs += [(i * 2 + 1, ((i - d) % 4) * 2 + 1) for i in range(4)]
    return lax.ppermute(value, (axis, "core"), pairs)


def chip_perm(k):
    pairs = []
    for z in range(2):
        for x in range(4):
            at = (z * 4 + x) * 2
            if k:
                pairs.append((at, (z * 4 + (x + k) % 4) * 2))
            pairs.append((at + 1, ((1 - z) * 4 + (x - k) % 4) * 2 + 1))
    return pairs


def body(out_grad, preact, aggregated, weight, tiles, tile_coords, tile_count):
    smem, vmem, hbm = spec(pltpu.SMEM), spec(), spec(pltpu.HBM)
    nodes = out_grad.shape[0]
    pos = jnp.stack([lax.axis_index(a) for a in ROWS + COLS]).astype(i32)
    inputs = jnp.concatenate([out_grad, preact, aggregated, weight], 0)
    swap = [(0, 1), (1, 0)]
    local = call(local_kernel, struct(2 * T, nodes), [vmem])(inputs)
    mine = call(chip_kernel, struct(2 * T + 64, nodes), [smem, vmem, vmem])(
        pos, local, lax.ppermute(local, "core", swap)
    )
    order, held = call(
        order_kernel,
        [pltpu.SMEM((1, PLACES), i32), pltpu.VMEM((SLOTS, T, T), bf16)],
        [smem, smem, hbm, hbm],
        [pltpu.SMEM((2, SLOTS), i32), pltpu.SemaphoreType.DMA((1 + SLOTS // PART,))],
        pl.CostEstimate(flops=0, bytes_accessed=2 * SLOTS * T * T * 2, transcendentals=0),
        (smem, vmem),
    )(
        pos,
        tile_count.reshape(1),
        pltpu.with_memory_space_constraint(tile_coords.reshape(2, SLOTS), pltpu.HBM),
        pltpu.with_memory_space_constraint(tiles.reshape(SLOTS, T, T), pltpu.HBM),
    )
    got = [lax.ppermute(mine, COLS, chip_perm(k)) for k in range(4)]
    swapped = []
    for k in range(4):
        ready = got[k]
        if k == 0:
            ready, _ = lax.optimization_barrier((ready, order))
        swapped.append(lax.ppermute(ready, "core", swap))
    cost = lambda share: pl.CostEstimate(
        flops=share * SLOTS * 2 * T**3, bytes_accessed=share * SLOTS * T * T * 2, transcendentals=0
    )
    early, late, onward = struct(5 * T, T), struct(4 * T, T), struct(3 * T, T)
    grads, weight_part, early_2, late_2 = call(
        first_kernel,
        [struct(BLOCKS, T, T), struct(T, T), early, late],
        [smem] * 2 + [vmem] * 10,
        [pltpu.VMEM((9, T, T), f32), pltpu.VMEM((8, 64, 2 * T), bf16)],
        cost(1),
    )(pos, order, mine, *got, *swapped, held)
    early_1, late_1, early_3, late_3 = call(
        second_kernel,
        [early, late] * 2,
        [smem] + [vmem] * 3,
        [pltpu.VMEM((17, T, T), f32)],
        cost(1),
    )(order, grads, weight_part, held)
    own_early, own_late = call(
        third_kernel,
        [struct(4 * T, T, dtype=f32)] * 2,
        [smem] + [vmem] * 2 + [spec(pl.ANY)],
        [pltpu.VMEM((9, T, T), f32)],
        cost(1),
    )(order, grads, held, early_1)
    got_early = [around("y", v, d) for d, v in ((1, early_1), (2, early_2), (3, early_3))]
    got_late = [around("y", v, d) for d, v in ((1, late_1), (2, late_2), (3, late_3))]
    send_2, send_3, weight_y = call(
        early_kernel, [onward, onward, struct(T, T)], [vmem] * 5, cost=cost(10)
    )(own_early, weight_part, *got_early)
    z_2, z_3 = around("zh", send_2, 2), around("zh", send_3, 3)
    keep, send_1 = call(late_kernel, [struct(2 * T, T, dtype=f32), onward], [vmem] * 5)(
        own_late, weight_y, *got_late
    )
    z_1 = around("zh", send_1, 1)
    devices = 1
    for a in ROWS + COLS:
        devices *= lax.axis_size(a)
    scale = 1.0 / (nodes * devices) ** 0.5
    input_grad, weight_grad = call(
        functools.partial(z_kernel, scale),
        [struct(nodes, T), struct(T, T, dtype=f32)],
        [vmem] * 5,
    )(keep, weight_y, z_1, z_2, z_3)
    return input_grad, weight_grad


def solution(mesh):
    fine = Mesh(mesh.devices.reshape(4, 4, 2, 4, 2), ROWS + COLS)
    every = ROWS + COLS
    return jax.shard_map(
        body,
        mesh=fine,
        in_specs=(
            P(every, None),
            P(every, None),
            P(every, None),
            P(),
            P(ROWS, COLS, None, None, None),
            P(ROWS, COLS, None, None),
            P(ROWS, COLS),
        ),
        out_specs=(P(every, None), P()),
        check_vma=False,
    )
```
